32 devices in a mesh: seq: 8 (over y, x, core), dp: 4 (over z).
Axes of the slice: x: 2, y: 2, z: 4, core: 2. Of those that a mesh axis runs over, the one named last changes fastest.
Arguments:
- tokens: bfloat16 [4, 6144, 1024], P('dp', 'seq'), may hold values from -6 to 6
- cotangent: bfloat16 [4, 6144, 1024], P('dp', 'seq'), may hold values from -6 to 6
- lengths: int32 [4, 4], P('dp'), may hold values from 768 to 3072, as said below
- attend_weight: float32 [1024, 3072], P('seq'), may hold values from -0.1875 to 0.1875
- merge_weight: float32 [1024, 1024], P('seq'), may hold values from -0.75 to 0.75
- expand_weight: float32 [1024, 4096], P('seq'), may hold values from -0.1875 to 0.1875
- shrink_weight: float32 [4096, 1024], P('seq'), may hold values from -0.09375 to 0.09375
- gains_biases: float32 [13312], P('seq'), may hold values from -0.8 to 2.25
- attend_first: float32 [1024, 3072], P('seq'), may hold values from -10 to 10
- attend_second: float32 [1024, 3072], P('seq'), may hold values from 0.24576 to 0.98304
- merge_first: float32 [1024, 1024], P('seq'), may hold values from -32 to 32
- merge_second: float32 [1024, 1024], P('seq'), may hold values from 2.21184 to 8.84736
- expand_first: float32 [1024, 4096], P('seq'), may hold values from -32 to 32
- expand_second: float32 [1024, 4096], P('seq'), may hold values from 2.21184 to 8.84736
- shrink_first: float32 [4096, 1024], P('seq'), may hold values from -64 to 64
- shrink_second: float32 [4096, 1024], P('seq'), may hold values from 8.84736 to 35.38944
- vector_first: float32 [13312], P('seq'), may hold values from -112 to 112
- vector_second: float32 [13312], P('seq'), may hold values from 24.576 to 98.304
Outputs:
- block_output: bfloat16 [4, 6144, 1024], P('dp', 'seq')
- input_grad: bfloat16 [4, 6144, 1024], P('dp', 'seq')
- attend_new: float32 [1024, 3072], P('seq')
- attend_mean: float32 [1024, 3072], P('seq')
- attend_square: float32 [1024, 3072], P('seq')
- merge_new: float32 [1024, 1024], P('seq')
- merge_mean: float32 [1024, 1024], P('seq')
- merge_square: float32 [1024, 1024], P('seq')
- expand_new: float32 [1024, 4096], P('seq')
- expand_mean: float32 [1024, 4096], P('seq')
- expand_square: float32 [1024, 4096], P('seq')
- shrink_new: float32 [4096, 1024], P('seq')
- shrink_mean: float32 [4096, 1024], P('seq')
- shrink_square: float32 [4096, 1024], P('seq')
- vector_new: float32 [13312], P('seq')
- vector_mean: float32 [13312], P('seq')
- vector_square: float32 [13312], P('seq')
- trust_norms: float32 [10], replicated
The draws below stay inside these ranges and needn't reach their ends.
Inputs may be any that keep to these rules, and one draw needn't show every extreme that they name: Each row lists the lengths of its group's 4 sequences in order; they sum to 6144, and every row has one entry of exactly 768 and one of exactly 3072.
All inputs are finite; a program needn't handle non-finite values.
Results may differ from the reference program's by a relative error of at most 0.006.
The reference program's roundings to bfloat16 on the way count: a program that leaves them out, or rounds other values in their place, can miss the bound.
Values may be sent and summed in bfloat16 or wider, within the bound.
No kernel may reach another device: no remote copies, remote signals or barrier semaphores. Data moves between devices by JAX's collectives and lax.ppermute only.
A program may use at most 384 MiB of HBM per device.

```python
import math
import jax
import jax.numpy as jnp
import numpy as np
from jax import lax

D = 1024
FF = 4096
H = 16
HEAD = 64
ROT = 16
FEAT = 64
SPAN = 64
NDOCS = 4
STEP = 10
GROUP = 6144
SHORT = 768
LONG = 3072
GROUPS = 4
NTOK = 24576
NVEC = 13312


def draw_lengths(key, part):
    key = jax.random.fold_in(key, 11)
    split_key, order_key = jax.random.split(key)
    rest = GROUP - SHORT - LONG
    first = jax.random.randint(split_key, (GROUPS,), SHORT, rest - SHORT + 1).astype(jnp.int32)
    base = jnp.stack([jnp.full((GROUPS,), SHORT, jnp.int32), jnp.full((GROUPS,), LONG, jnp.int32), first, rest - first], 1)
    scores = jax.random.randint(order_key, (GROUPS, NDOCS), 0, 1 << 20).astype(jnp.int32) * NDOCS + jnp.arange(NDOCS, dtype=jnp.int32)[None, :]
    order = jnp.argsort(scores, axis=1, stable=True).astype(jnp.int32)
    return jnp.take_along_axis(base, order, 1).astype(jnp.int32)


def draw_gains_biases(key, part):
    key = jax.random.fold_in(key, 23)
    gain_key, bias_key, rest_key = jax.random.split(key, 3)
    ramp = 0.6 + 1.2 * jnp.arange(D, dtype=jnp.float32) / D
    gains = ramp[None, :] * jax.random.uniform(gain_key, (2, D), jnp.float32, 0.8, 1.25)
    shifts = jnp.clip(0.2 * jax.random.normal(bias_key, (2, D), jnp.float32), -0.8, 0.8)
    others = jnp.clip(0.2 * jax.random.normal(rest_key, (5 * D + FF,), jnp.float32), -0.8, 0.8)
    return jnp.concatenate([gains[0], shifts[0], gains[1], shifts[1], others])


def level_of(rng, dims, cuts, low, largest):
    loudness = 1.0
    for position, blocks in cuts:
        draws = jax.random.uniform(jax.random.fold_in(jax.random.fold_in(rng, 6), position), (blocks,), jnp.float32, low / len(cuts), largest / len(cuts))
        loudness = loudness * jnp.repeat(jnp.exp(draws), dims[position] // blocks).reshape((-1,) + (1,) * (len(dims) - 1 - position))
    return loudness


def normal_values(key, shape, width, most, shards=(), kind=jnp.bfloat16):
    loudness = level_of(key, shape, shards, -0.22, 0.18) if shards else 1.0
    values = jax.random.normal(key, shape, jnp.float32) * width * loudness
    return jnp.minimum(jnp.maximum(values, -most), most).astype(kind)


def setup_inputs(seed: int = 0) -> dict:
    streams_of = jax.random.split(jax.random.key(seed), 19)
    tokens = normal_values(streams_of[0], (GROUPS, GROUP, D), 1.0, 6.0, ((0, 4), (1, 8)))
    cotangent = normal_values(streams_of[1], (GROUPS, GROUP, D), 1.0, 6.0, ((0, 4), (1, 8)))
    lengths = draw_lengths(jax.random.fold_in(streams_of[18], 71), 0)
    attend_weight = normal_values(streams_of[3], (D, 3 * D), D ** -0.5, 0.1875, ((0, 8),), jnp.float32)
    merge_weight = normal_values(streams_of[4], (D, D), (D // 16) ** -0.5, 0.75, ((0, 8),), jnp.float32)
    expand_weight = normal_values(streams_of[5], (D, FF), D ** -0.5, 0.1875, ((0, 8),), jnp.float32)
    shrink_weight = normal_values(streams_of[6], (FF, D), FF ** -0.5, 0.09375, ((0, 8),), jnp.float32)
    gains_biases = draw_gains_biases(jax.random.fold_in(streams_of[18], 71), 0)
    attend_first = normal_values(streams_of[8], (D, 3 * D), (0.011 * NTOK ** 0.5), 10.0, ((0, 8),), jnp.float32)
    attend_second = jnp.clip(jnp.exp(math.log(0.98304) - 1.3862944 * jax.random.uniform(streams_of[9], (D, 3 * D), jnp.float32) ** level_of(streams_of[9], (D, 3 * D), ((0, 8),), -0.2, 0.2)), 0.24576, 0.98304)
    merge_first = normal_values(streams_of[10], (D, D), (0.033 * NTOK ** 0.5), 32.0, ((0, 8),), jnp.float32)
    merge_second = jnp.clip(jnp.exp(math.log(8.84736) - 1.3862944 * jax.random.uniform(streams_of[11], (D, D), jnp.float32) ** level_of(streams_of[11], (D, D), ((0, 8),), -0.2, 0.2)), 2.21184, 8.84736)
    expand_first = normal_values(streams_of[12], (D, FF), (0.033 * NTOK ** 0.5), 32.0, ((0, 8),), jnp.float32)
    expand_second = jnp.clip(jnp.exp(math.log(8.84736) - 1.3862944 * jax.random.uniform(streams_of[13], (D, FF), jnp.float32) ** level_of(streams_of[13], (D, FF), ((0, 8),), -0.2, 0.2)), 2.21184, 8.84736)
    shrink_first = normal_values(streams_of[14], (FF, D), (0.066 * NTOK ** 0.5), 64.0, ((0, 8),), jnp.float32)
    shrink_second = jnp.clip(jnp.exp(math.log(35.38944) - 1.3862944 * jax.random.uniform(streams_of[15], (FF, D), jnp.float32) ** level_of(streams_of[15], (FF, D), ((0, 8),), -0.2, 0.2)), 8.84736, 35.38944)
    vector_first = normal_values(streams_of[16], (NVEC,), (0.11 * NTOK ** 0.5), 112.0, ((0, 8),), jnp.float32)
    vector_second = jnp.clip(jnp.exp(math.log(98.304) - 1.3862944 * jax.random.uniform(streams_of[17], (NVEC,), jnp.float32) ** level_of(streams_of[17], (NVEC,), ((0, 8),), -0.2, 0.2)), 24.576, 98.304)
    return dict(tokens=tokens, cotangent=cotangent, lengths=lengths, attend_weight=attend_weight, merge_weight=merge_weight, expand_weight=expand_weight, shrink_weight=shrink_weight, gains_biases=gains_biases, attend_first=attend_first, attend_second=attend_second, merge_first=merge_first, merge_second=merge_second, expand_first=expand_first, expand_second=expand_second, shrink_first=shrink_first, shrink_second=shrink_second, vector_first=vector_first, vector_second=vector_second)


precise = lax.Precision.HIGHEST
SCALE = 0.25
BASE = 10000.0
BETA_ONE = 0.9
BETA_TWO = 0.999
EPSILON = 1e-06
DECAY = 0.01
RATE = 0.25

@jax.custom_vjp
def low(v):
    return lax.optimization_barrier(v.astype(jnp.bfloat16)).astype(jnp.float32)

@jax.custom_vjp
def low_back(v):
    return v

def low_keep(v):
    return (low(v), None)

def low_pass(kept, grad):
    return (grad,)

def back_keep(v):
    return (v, None)

def back_low(kept, grad):
    return (low(grad),)
low.defvjp(low_keep, low_pass)
low_back.defvjp(back_keep, back_low)

def feature_tables(head, feats):
    row_index = np.arange(head)[:, None]
    col_index = np.arange(head)[None, :]
    cosine = np.sqrt(2.0 / head) * np.cos(np.pi * (2 * col_index + 1) * row_index / (2.0 * head))
    cosine[0, :] = cosine[0, :] / np.sqrt(2.0)
    entry = np.arange(head)[:, None] + 1.0
    column = np.arange(feats)[None, :] + 0.5
    first_point = np.clip(np.mod(column / feats + entry * 0.7548776662, 1.0), 0.01, 0.99)
    second_point = np.mod(column * 0.569840291 + entry * 0.6180339887, 1.0)
    omega = np.sqrt(-2.0 * np.log(first_point)) * np.cos(2.0 * np.pi * second_point)
    matrix = cosine.T @ omega * SCALE
    weighting = (1.5 + np.cos(2.0 * np.pi * column[0] / feats)) / (1.5 * feats)
    return (matrix.astype(np.float32), weighting.astype(np.float32))

def features(heads_in):
    matrix, weighting = feature_tables(HEAD, FEAT)
    project = jnp.einsum('...e,ef->...f', heads_in, jnp.asarray(matrix), precision=precise)
    squares = SCALE * SCALE * lax.optimization_barrier(jnp.sum(heads_in * heads_in, -1, keepdims=True))
    return jnp.asarray(weighting) * jnp.exp(project - 0.5 * squares)

def layer_norm(inputs, gain, shift):
    center = inputs - lax.optimization_barrier(jnp.mean(inputs, -1, keepdims=True))
    spread = lax.optimization_barrier(jnp.mean(center * center, -1, keepdims=True))
    return center * lax.rsqrt(spread + 1e-05) * gain + shift

def rotate(heads_in, offset):
    halfway = ROT // 2
    inverse = jnp.exp(jnp.arange(halfway, dtype=jnp.float32) * (-2.0 * math.log(BASE) / ROT))
    angles = offset.astype(jnp.float32)[..., None] * inverse
    cosine = jnp.cos(angles)[..., None, :]
    sines = jnp.sin(angles)[..., None, :]
    first_half = heads_in[..., :halfway]
    second_half = heads_in[..., halfway:ROT]
    return jnp.concatenate([first_half * cosine - second_half * sines, second_half * cosine + first_half * sines, heads_in[..., ROT:]], -1)

def linear_attention(qkv, offset, segment):
    pieces = qkv.reshape(GROUPS, GROUP, 3, H, HEAD)
    queries = features(rotate(pieces[:, :, 0], offset))
    key_feats = features(rotate(pieces[:, :, 1], offset))
    values = pieces[:, :, 2]
    count = GROUP // SPAN

    def blocks(array):
        return jnp.moveaxis(array.reshape((GROUPS, count, SPAN) + array.shape[2:]), 1, 0)
    inner = jnp.arange(SPAN)[:, None] >= jnp.arange(SPAN)[None, :]

    def advance(carry, block):
        state, key_total, before = carry
        query_feat, key_feat, value_rows, labels = block
        causal = (inner[None] & (labels[:, :, None] == labels[:, None, :])).astype(jnp.float32)
        scores = jnp.einsum('gthf,gshf->ghts', query_feat, key_feat, precision=precise) * causal[:, None]
        reach = (labels == before[:, None]).astype(jnp.float32)
        weighted = jnp.einsum('ghts,gshe->gthe', scores, value_rows, precision=precise)
        weighted = weighted + reach[:, :, None, None] * jnp.einsum('gthf,ghfe->gthe', query_feat, state, precision=precise)
        totals = jnp.transpose(lax.optimization_barrier(jnp.sum(scores, -1)), (0, 2, 1))
        totals = totals + reach[:, :, None] * jnp.einsum('gthf,ghf->gth', query_feat, key_total, precision=precise)
        final = labels[:, -1]
        keeping = (final == before).astype(jnp.float32)
        tailing = (labels == final[:, None]).astype(jnp.float32)
        kept = key_feat * tailing[:, :, None, None]
        state = keeping[:, None, None, None] * state + jnp.einsum('gthf,gthe->ghfe', kept, value_rows, precision=precise)
        key_total = keeping[:, None, None] * key_total + lax.optimization_barrier(jnp.sum(kept, 1))
        return ((state, key_total, final), weighted / totals[..., None])
    start = (jnp.zeros((GROUPS, H, FEAT, HEAD), jnp.float32), jnp.zeros((GROUPS, H, FEAT), jnp.float32), jnp.zeros((GROUPS,), jnp.int32))
    _, outcome = lax.scan(jax.checkpoint(advance), start, (blocks(queries), blocks(key_feats), blocks(values), blocks(segment)))
    return jnp.moveaxis(outcome, 0, 1).reshape(GROUPS, GROUP, D)

def lamb_update(master, first, second, grad, decay):
    first = BETA_ONE * first + (1.0 - BETA_ONE) * grad
    second = BETA_TWO * second + (1.0 - BETA_TWO) * grad * grad
    update = first / (1.0 - BETA_ONE ** STEP) / (jnp.sqrt(second / (1.0 - BETA_TWO ** STEP)) + EPSILON) + decay * master
    return (first, second, update)

def reference(tokens, cotangent, lengths, attend_weight, merge_weight, expand_weight, shrink_weight, gains_biases, attend_first, attend_second, merge_first, merge_second, expand_first, expand_second, shrink_first, shrink_second, vector_first, vector_second):
    masters = (attend_weight, merge_weight, expand_weight, shrink_weight, gains_biases)
    rounded = tuple((master.astype(jnp.bfloat16).astype(jnp.float32) for master in masters))
    positions = jnp.arange(GROUP, dtype=jnp.int32)
    bounds = jnp.cumsum(lengths, axis=1).astype(jnp.int32)
    passed = bounds[:, None, :] <= positions[None, :, None]
    segment = lax.optimization_barrier(jnp.sum(passed.astype(jnp.int32), -1)).astype(jnp.int32)
    starts = lax.optimization_barrier(jnp.sum(jnp.where(passed, lengths[:, None, :], 0), -1)).astype(jnp.int32)
    offset = positions[None, :] - starts

    def forward(inputs, attend, merge, expand, shrink, vector):
        gain_one = vector[0:D]
        shift_one = vector[D:2 * D]
        gain_two = vector[2 * D:3 * D]
        shift_two = vector[3 * D:4 * D]
        bias_attend = vector[4 * D:7 * D]
        bias_merge = vector[7 * D:8 * D]
        bias_expand = vector[8 * D:8 * D + FF]
        bias_shrink = vector[8 * D + FF:]
        normed_one = low(layer_norm(inputs, gain_one, shift_one))
        normed_two = low(layer_norm(inputs, gain_two, shift_two))
        qkv = low_back(jnp.einsum('gnd,de->gne', normed_one, attend, precision=precise) + bias_attend)
        mixed = low(linear_attention(qkv, offset, segment))
        before_act = low_back(jnp.einsum('gnd,de->gne', normed_two, expand, precision=precise) + bias_expand)
        active = low(jax.nn.gelu(before_act, approximate=False))
        result = inputs + jnp.einsum('gnd,de->gne', mixed, merge, precision=precise) + bias_merge
        return result + jnp.einsum('gnf,fd->gnd', active, shrink, precision=precise) + bias_shrink
    inputs = tokens.astype(jnp.float32)
    output, pullback = jax.vjp(forward, inputs, *rounded)
    grads = pullback(cotangent.astype(jnp.float32))
    firsts = (attend_first, merge_first, expand_first, shrink_first, vector_first)
    seconds = (attend_second, merge_second, expand_second, shrink_second, vector_second)
    decays = (DECAY, DECAY, DECAY, DECAY, 0.0)
    results = []
    weight_norms = []
    update_norms = []
    for master, first, second, grad, decay in zip(masters, firsts, seconds, grads[1:], decays):
        first, second, update = lamb_update(master, first, second, grad, decay)
        weight_norm = jnp.sqrt(jnp.sum(master * master))
        update_norm = jnp.sqrt(jnp.sum(update * update))
        fresh = master - RATE * (weight_norm / (update_norm + EPSILON)) * update
        results.extend([fresh, first, second])
        weight_norms.append(weight_norm)
        update_norms.append(update_norm)
    trust_norms = jnp.stack(weight_norms + update_norms)
    return (output.astype(jnp.bfloat16), grads[0].astype(jnp.bfloat16), results[0], results[1], results[2], results[3], results[4], results[5], results[6], results[7], results[8], results[9], results[10], results[11], results[12], results[13], results[14], trust_norms)
```

```python
import math

import jax
import jax.numpy as jnp
import ml_dtypes
import numpy as np
from jax import lax
from jax.experimental import pallas as pl
from jax.experimental.pallas import tpu as pltpu
from jax.sharding import PartitionSpec as P

D = 1024
FF = 4096
H = 16
HEAD = 64
ROT = 16
FEAT = 64
STEP = 10

SCALE = 0.25
BASE = 10000.0
BETA_ONE = 0.9
BETA_TWO = 0.999
EPSILON = 1e-06
DECAY = 0.01
RATE = 0.25

CHUNK = 256
LANES = 256
EACH = LANES // HEAD
NGROUP = D // LANES
STATE = HEAD + 8
ROOM = 56 * 1024 * 1024
f32 = jnp.float32
bf16 = jnp.bfloat16


def feature_tables(head, feats):
    row_index = np.arange(head)[:, None]
    col_index = np.arange(head)[None, :]
    cosine = np.sqrt(2.0 / head) * np.cos(np.pi * (2 * col_index + 1) * row_index / (2.0 * head))
    cosine[0, :] = cosine[0, :] / np.sqrt(2.0)
    entry = np.arange(head)[:, None] + 1.0
    column = np.arange(feats)[None, :] + 0.5
    first_point = np.clip(np.mod(column / feats + entry * 0.7548776662, 1.0), 0.01, 0.99)
    second_point = np.mod(column * 0.569840291 + entry * 0.6180339887, 1.0)
    omega = np.sqrt(-2.0 * np.log(first_point)) * np.cos(2.0 * np.pi * second_point)
    matrix = cosine.T @ omega * SCALE
    weighting = (1.5 + np.cos(2.0 * np.pi * column[0] / feats)) / (1.5 * feats)
    return (matrix.astype(np.float32), weighting.astype(np.float32))


def group_tables():
    matrix, weighting = feature_tables(HEAD, FEAT)
    eye = np.eye(EACH, dtype=np.float32)
    wide = np.kron(eye, matrix)
    high = wide.astype(ml_dtypes.bfloat16)
    low = (wide - high.astype(np.float32)).astype(ml_dtypes.bfloat16)
    ones = np.kron(eye, np.ones((HEAD, HEAD), np.float32)).astype(ml_dtypes.bfloat16)
    return np.stack([high, low, ones]), np.tile(weighting, EACH)[None, :]


def dot_nn(a, b):
    return lax.dot_general(a, b, (((1,), (0,)), ((), ())), preferred_element_type=f32)


def dot_nt(a, b):
    return lax.dot_general(a, b, (((1,), (1,)), ((), ())), preferred_element_type=f32)


def dot_tn(a, b):
    return lax.dot_general(a, b, (((0,), (0,)), ((), ())), preferred_element_type=f32)


def halves(value):
    high = value.astype(bf16)
    return high, (value - high.astype(f32)).astype(bf16)


def dot_three(dot, high, low, other_high, other_low):
    return dot(high, other_high) + dot(low, other_high) + dot(high, other_low)


def twice(table):
    return jnp.concatenate([table, table], axis=1)


def flat(value):
    return value.reshape(-1, value.shape[-1])


def head_mask(index, dtype):
    lane = lax.broadcasted_iota(jnp.int32, (1, LANES), 1)
    inside = (lane >= index * HEAD) & (lane < (index + 1) * HEAD)
    return jnp.where(inside, 1.0, 0.0).astype(dtype)


def turn(value, table_ref):
    cosine, first, second = (twice(table_ref[i]) for i in range(3))
    half = ROT // 2
    return (
        value * cosine
        + pltpu.roll(value, LANES - half, 1) * first
        + pltpu.roll(value, half, 1) * second
    )


def turn_back(grad, table_ref):
    cosine, first, second = (twice(table_ref[i]) for i in range(3))
    half = ROT // 2
    return (
        grad * cosine
        + pltpu.roll(grad * first, half, 1)
        + pltpu.roll(grad * second, LANES - half, 1)
    )


def phi(value, const_ref, weight_ref):
    high, low = halves(value)
    project = (
        dot_nn(high, const_ref[0]) + dot_nn(low, const_ref[0]) + dot_nn(high, const_ref[1])
    )
    top, rest = halves(value * value)
    squares = dot_nn(top, const_ref[2]) + dot_nn(rest, const_ref[2])
    return weight_ref[...] * jnp.exp(project - (0.5 * SCALE * SCALE) * squares)


def phi_back(grad, feats, value, const_ref):
    high, low = halves(grad * feats)
    project = (
        dot_nt(high, const_ref[0]) + dot_nt(low, const_ref[0]) + dot_nt(high, const_ref[1])
    )
    total = dot_nn(high, const_ref[2]) + dot_nn(low, const_ref[2])
    return project - (SCALE * SCALE) * value * total


def spread(state_ref, const_ref):
    packed = state_ref[0:HEAD, :]
    tall = jnp.concatenate([packed] * EACH, axis=0)
    return tall * const_ref[2].astype(f32)


def squeeze_state(state):
    total = state[0:HEAD]
    for index in range(1, EACH):
        total = total + state[index * HEAD : (index + 1) * HEAD]
    return total


def qkv_kernel(
    h_ref, wq_ref, wk_ref, wv_ref, b_ref, table_ref, marks_ref, const_ref, weight_ref,
    q_ref, k_ref, v_ref, vl_ref, uq_ref, uk_ref, s_ref,
):
    rows = h_ref[...]
    query = turn(dot_nn(rows, flat(wq_ref[...])) + b_ref[0:1, :], table_ref)
    uq_ref[...] = query.astype(bf16)
    q_ref[...] = phi(query, const_ref, weight_ref).astype(bf16)
    key = turn(dot_nn(rows, flat(wk_ref[...])) + b_ref[1:2, :], table_ref)
    uk_ref[...] = key.astype(bf16)
    feats = phi(key, const_ref, weight_ref).astype(bf16)
    k_ref[...] = feats
    value, value_low = halves(dot_nn(rows, flat(wv_ref[...])) + b_ref[2:3, :])
    v_ref[...] = value
    vl_ref[...] = value_low
    segment = twice(table_ref[3])
    tail = jnp.where(segment == marks_ref[15:16, :], 1.0, 0.0)
    kept = feats.astype(f32) * tail
    kept_low = kept.astype(bf16)
    state = (dot_tn(kept_low, value) + dot_tn(kept_low, value_low)) * const_ref[2].astype(f32)
    s_ref[0:HEAD, :] = squeeze_state(state)
    s_ref[HEAD:STATE, :] = jnp.broadcast_to(jnp.sum(kept, 0, keepdims=True), (8, LANES))


def attend_kernel(
    q_ref, k_ref, v_ref, vl_ref, uq_ref, s_ref, g_ref, wm_ref, table_ref, row_ref, marks_ref, const_ref, core_ref,
    mixed_ref, dq_ref, dk_ref, dv_ref, ds_ref, bias_ref, out_ref, send_ref, keep_ref,
    dnum_ref, dlow_ref, dden_ref,
):
    count = q_ref.shape[0] // CHUNK
    merge = flat(wm_ref[...])
    state = spread(s_ref, const_ref)
    total = s_ref[HEAD : HEAD + 1, :]
    blocks = const_ref[2].astype(f32)
    masks = [head_mask(index, bf16) for index in range(EACH)]
    lower = lax.broadcasted_iota(jnp.int32, (CHUNK, CHUNK), 0) >= lax.broadcasted_iota(
        jnp.int32, (CHUNK, CHUNK), 1
    )
    bias = jnp.zeros((1, LANES), f32)
    for c in range(count):
        here = pl.ds(c * CHUNK, CHUNK)
        query, key = q_ref[here, :], k_ref[here, :]
        value, value_low = v_ref[here, :], vl_ref[here, :]
        segment = twice(table_ref[3, here, :])
        before, final = marks_ref[c : c + 1, :], marks_ref[8 + c : 9 + c, :]
        reach = jnp.where(segment == before, 1.0, 0.0)
        tail = jnp.where(segment == final, 1.0, 0.0)
        keep = jnp.where(final == before, 1.0, 0.0)
        causal = lower & (segment == row_ref[0:1, c * CHUNK : (c + 1) * CHUNK])
        grad_mixed = dot_nt(g_ref[here, :], merge)
        state_high, state_low = halves(state)
        reached = query * reach.astype(bf16)
        number = dot_nn(reached, state_high) + dot_nn(reached, state_low)
        top, rest = halves(reached.astype(f32) * total)
        totals = dot_nn(top, const_ref[2]) + dot_nn(rest, const_ref[2])
        scores = []
        for index in range(EACH):
            mask = masks[index]
            score = jnp.where(causal, dot_nt(query, key * mask), 0.0)
            totals = totals + jnp.sum(score, 1, keepdims=True) * mask.astype(f32)
            high, low = halves(score)
            scores.append((high, low))
            number = number + dot_three(dot_nn, high, low, value * mask, value_low * mask)
        mixed = number / totals
        mixed_ref[here, :] = mixed.astype(bf16)
        slope_number = grad_mixed / totals
        dnum, dlow = halves(slope_number)
        dnum_ref[here, :] = dnum
        dlow_ref[here, :] = dlow
        top, rest = halves(slope_number * mixed)
        dden = -(dot_nn(top, const_ref[2]) + dot_nn(rest, const_ref[2]))
        dden_ref[here, :] = dden
        grad_query = reach * (
            dot_three(dot_nt, dnum, dlow, state_high, state_low) + dden * total
        )
        grad_key = jnp.zeros((CHUNK, LANES), f32)
        grad_value = jnp.zeros((CHUNK, LANES), f32)
        for index in range(EACH):
            mask = masks[index]
            column = dden[:, index * HEAD : index * HEAD + 1]
            slope = dot_three(dot_nt, dnum, dlow, value * mask, value_low * mask) + column
            high, low = halves(jnp.where(causal, slope, 0.0))
            grad_query = grad_query + dot_nn(high, key * mask) + dot_nn(low, key * mask)
            grad_key = grad_key + dot_tn(high, query * mask) + dot_tn(low, query * mask)
            high, low = scores[index]
            grad_value = grad_value + dot_three(dot_tn, high, low, dnum * mask, dlow * mask)
        dk_ref[here, :] = grad_key
        dv_ref[here, :] = grad_value
        grad = phi_back(grad_query, query.astype(f32), uq_ref[here, :].astype(f32), const_ref)
        grad = turn_back(grad, table_ref.at[:, here, :]).astype(bf16)
        dq_ref[here, :] = grad
        bias = bias + jnp.sum(grad.astype(f32), 0, keepdims=True)
        if c < count - 1:
            kept = key.astype(f32) * tail
            kept_low = kept.astype(bf16)
            state = keep * state + blocks * (dot_tn(kept_low, value) + dot_tn(kept_low, value_low))
            total = keep * total + jnp.sum(kept, 0, keepdims=True)
    bias_ref[...] = jnp.broadcast_to(bias, (8, LANES))
    grad_state = jnp.zeros((LANES, LANES), f32)
    grad_total = jnp.zeros((1, LANES), f32)
    for c in reversed(range(count)):
        here = pl.ds(c * CHUNK, CHUNK)
        segment = twice(table_ref[3, here, :])
        before, final = marks_ref[c : c + 1, :], marks_ref[8 + c : 9 + c, :]
        reach = jnp.where(segment == before, 1.0, 0.0)
        tail = jnp.where(segment == final, 1.0, 0.0)
        keep = jnp.where(final == before, 1.0, 0.0)
        if c < count - 1:
            high, low = halves(grad_state)
            dk_ref[here, :] += tail * (
                dot_three(dot_nt, v_ref[here, :], vl_ref[here, :], high, low) + grad_total
            )
            dv_ref[here, :] += tail * (dot_nn(k_ref[here, :], high) + dot_nn(k_ref[here, :], low))
        reached = q_ref[here, :].astype(f32) * reach
        low_reached = reached.astype(bf16)
        grad_state = keep * grad_state + blocks * (
            dot_tn(low_reached, dnum_ref[here, :]) + dot_tn(low_reached, dlow_ref[here, :])
        )
        grad_total = keep * grad_total + jnp.sum(reached * dden_ref[here, :], 0, keepdims=True)
    ds_ref[0:HEAD, :] = squeeze_state(grad_state)
    ds_ref[HEAD:STATE, :] = jnp.broadcast_to(grad_total, (8, LANES))
    mixed = mixed_ref[...]
    accumulate(out_ref, dot_nn(mixed, merge))
    part_owners(dot_tn(mixed, g_ref[...]), core_ref, send_ref, keep_ref)


def accumulate(ref, value):
    first = pl.program_id(0) == 0

    @pl.when(first)
    def _():
        ref[...] = value

    @pl.when(jnp.logical_not(first))
    def _():
        ref[...] += value


def part_owners(value, core_ref, send_ref, keep_ref):
    held = send_ref.shape
    pairs = value.reshape((held[0], 2) + held[1:]).astype(send_ref.dtype)
    even, odd = pairs[:, 0], pairs[:, 1]
    first = core_ref[0] == 0
    keep, send = jnp.where(first, even, odd), jnp.where(first, odd, even)
    keep_ref[...], send_ref[...] = keep, send


def finish_kernel(
    k_ref, v_ref, vl_ref, uk_ref, dq_ref, dk_ref, dv_ref, ds_ref, table_ref, marks_ref, const_ref,
    wq_ref, wk_ref, wv_ref, ht_ref, core_ref, sent_ref, kept_ref, done_ref,
    bias_ref, dh_ref, send_ref, keep_ref,
):
    segment = twice(table_ref[3])
    tail = jnp.where(segment == marks_ref[15:16, :], 1.0, 0.0)
    high, low = halves(spread(ds_ref, const_ref))
    key, value = k_ref[...], v_ref[...]
    grad_key = dk_ref[...] + tail * (
        dot_three(dot_nt, value, vl_ref[...], high, low) + ds_ref[HEAD : HEAD + 1, :]
    )
    grad_value = dv_ref[...] + tail * (dot_nn(key, high) + dot_nn(key, low))
    grad = phi_back(grad_key, key.astype(f32), uk_ref[...].astype(f32), const_ref)
    grad = turn_back(grad, table_ref).astype(bf16)
    low_value = grad_value.astype(bf16)
    bias_ref[0:8, :] = jnp.broadcast_to(jnp.sum(grad.astype(f32), 0, keepdims=True), (8, LANES))
    bias_ref[8:16, :] = jnp.broadcast_to(
        jnp.sum(low_value.astype(f32), 0, keepdims=True), (8, LANES)
    )
    grads = (dq_ref[...], grad, low_value)
    weights = (flat(wq_ref[...]), flat(wk_ref[...]), flat(wv_ref[...]))
    accumulate(dh_ref, sum(dot_nt(g, w) for g, w in zip(grads, weights)))
    first = core_ref[0] == 0
    for index, value in enumerate(grads):
        pairs = dot_nn(ht_ref[...], value).reshape(-1, 2, send_ref.shape[2], LANES)
        keep_ref[:, index] = jnp.where(first, pairs[:, 0], pairs[:, 1])
        send_ref[:, index] = jnp.where(first, pairs[:, 1], pairs[:, 0])


def normal_cdf(value):
    bell = jnp.exp(-0.5 * value * value)
    near = jnp.abs(value) * (0.3275911 * math.sqrt(0.5)) + 1.0
    guess = pl.reciprocal(near, approx=True)
    t = guess * (2.0 - near * guess)
    poly = 0.5 * 1.061405429
    for factor in (-1.453152027, 1.421413741, -0.284496736, 0.254829592):
        poly = poly * t + 0.5 * factor
    tail = poly * t * bell
    return jnp.where(value >= 0.0, 1.0 - tail, tail), bell


def feed_kernel(
    h_ref, ht_ref, g_ref, we_ref, ws_ref, be_ref, core_ref, done_ref,
    out_ref, dh_ref, bias_ref, *grad_refs,
):
    step = pl.program_id(0)
    grad_out = g_ref[...]
    expand, shrink = flat(we_ref[...]), flat(ws_ref[...])
    width = expand.shape[1]
    pre = dot_nn(h_ref[...], expand) + be_ref[...]
    cdf, bell = normal_cdf(pre)
    active = (pre * cdf).astype(bf16)
    slope = cdf + pre * bell * (1.0 / math.sqrt(2.0 * math.pi))
    grad = (dot_nt(grad_out, shrink) * slope).astype(bf16)
    bias_ref[...] = jnp.broadcast_to(
        jnp.sum(grad.astype(f32), 0, keepdims=True), bias_ref.shape
    )
    _, blocks, rows, _ = grad_refs[0].shape
    where = lax.rem(step, D // width)
    block = step // (D // width)
    lanes = pl.ds(pl.multiple_of(where * width, width), width)
    wide = dot_nn(ht_ref[...], grad).astype(bf16)
    tall = dot_tn(active, grad_out).astype(bf16).reshape(2, blocks // 2, rows, D)
    if len(grad_refs) == 1:
        grad_refs[0][:, block, :, lanes] = wide.reshape(-1, rows, width)
        grad_refs[0][pl.ds(2 * step, 2), blocks // 2 :] = tall
    else:
        send_ref, keep_ref = grad_refs
        first = core_ref[0] == 0
        pairs = wide.reshape(-1, 2, rows, width)
        keep_ref[:, block, :, lanes] = jnp.where(first, pairs[:, 0], pairs[:, 1])
        send_ref[:, block, :, lanes] = jnp.where(first, pairs[:, 1], pairs[:, 0])
        keep_ref[step, blocks // 2 :] = jnp.where(first, tall[0], tall[1])
        send_ref[step, blocks // 2 :] = jnp.where(first, tall[1], tall[0])
    accumulate(out_ref, dot_nn(active, shrink))
    accumulate(dh_ref, dot_nt(grad, expand))


def lamb_step(master, first, second, grad, mean_ref, square_ref, update_ref, norms_ref):
    first, second, update = lamb_update(master, first, second, grad, DECAY)
    mean_ref[...], square_ref[...], update_ref[...] = first, second, update
    for index, value in enumerate((master, update)):
        squares = jnp.sum((value * value).reshape(-1, 8, value.shape[-1]), 0)
        accumulate(norms_ref.at[index], squares)


def lamb_feed_kernel(
    ep_ref, em_ref, es_ref, eg_ref, sp_ref, sm_ref, ss_ref, sg_ref, *refs
):
    enorm_ref, snorm_ref, *outs = refs[-8:]
    lamb_step(ep_ref[...], em_ref[...], es_ref[...], eg_ref[0].astype(f32), *outs[:3], enorm_ref)
    lamb_step(sp_ref[...], sm_ref[...], ss_ref[...], sg_ref[...].astype(f32), *outs[3:], snorm_ref)


def lamb_attend_kernel(
    ap_ref, am_ref, as_ref, mp_ref, mm_ref, ms_ref, grad_ref,
    anorm_ref, mnorm_ref, *outs,
):
    step = pl.program_id(0)
    grad = grad_ref[step].astype(f32)
    grad = grad + jnp.where(step < 2, grad_ref[jnp.minimum(4 + step, 5)].astype(f32), 0.0)
    lamb_step(ap_ref[...], am_ref[...], as_ref[...], grad, *outs[:3], anorm_ref)

    @pl.when(step == 0)
    def _():
        grad = grad_ref[3].astype(f32)
        lamb_step(mp_ref[...], mm_ref[...], ms_ref[...], grad, *outs[3:], mnorm_ref)


def renew_kernel(squares_ref, *refs):
    count = len(refs) // 3
    for index in range(count):
        master_ref, update_ref, fresh_ref = refs[2 * index], refs[2 * index + 1], refs[2 * count + index]
        lanes = (1, master_ref.shape[-1])
        weight = jnp.sqrt(jnp.full(lanes, squares_ref[2 * index], f32))
        change = jnp.sqrt(jnp.full(lanes, squares_ref[2 * index + 1], f32))
        ratio = RATE * (weight / (change + EPSILON))
        fresh_ref[...] = master_ref[...] - ratio * update_ref[...]


def whole(shape):
    return pl.BlockSpec(shape, lambda g: (0,) * len(shape), pipeline_mode=pl.Buffered(1))


def total_of(shape):
    return pl.BlockSpec(shape, lambda g: (0,) * len(shape))


def scalar():
    return pl.BlockSpec(memory_space=pltpu.SMEM)


def columns(rows, width=LANES, offset=0):
    return pl.BlockSpec((rows, width), lambda g: (0, g + offset))


def shaped(shape, dtype):
    return jax.ShapeDtypeStruct(shape, dtype)


def params():
    return pltpu.CompilerParams(vmem_limit_bytes=ROOM, dimension_semantics=("arbitrary",))


def layer_parts(inputs):
    center = inputs - jnp.mean(inputs, -1, keepdims=True)
    spread_of = jnp.mean(center * center, -1, keepdims=True)
    root = lax.rsqrt(spread_of + 1e-05)
    return center * root, root


def lamb_update(master, first, second, grad, decay):
    first = BETA_ONE * first + (1.0 - BETA_ONE) * grad
    second = BETA_TWO * second + (1.0 - BETA_TWO) * grad * grad
    update = (
        first / (1.0 - BETA_ONE**STEP) / (jnp.sqrt(second / (1.0 - BETA_TWO**STEP)) + EPSILON)
        + decay * master
    )
    return (first, second, update)


def per_device(
    tokens,
    cotangent,
    lengths,
    attend_weight,
    merge_weight,
    expand_weight,
    shrink_weight,
    gains_biases,
    attend_first,
    attend_second,
    merge_first,
    merge_second,
    expand_first,
    expand_second,
    shrink_first,
    shrink_second,
    vector_first,
    vector_second,
):
    rows = tokens.shape[1]
    count = rows // CHUNK
    n = lax.axis_size("seq")
    device = lax.axis_index("seq")
    grad_out = cotangent[0]
    own = D // n
    parts = 2 if FF // n >= 256 else 1
    sub = FF // n // parts
    tall = FF // D // parts
    core = lax.rem(device, 2)
    core_ref = core[None].astype(jnp.int32)

    def gather(blocks):
        shard = jnp.concatenate([block.astype(bf16) for block in blocks], 0)
        full = lax.all_gather(shard, "seq", axis=0, tiled=False)
        return full.reshape(n, shard.shape[0] // own, own, D)

    def of_part(array, index):
        return jnp.concatenate(
            [array[:, (j * parts + index) * sub : (j * parts + index + 1) * sub] for j in range(n)], 1
        )

    attend = gather(
        [attend_weight[:, :D], attend_weight[:, D : 2 * D], attend_weight[:, 2 * D :], merge_weight]
    )
    feeds = []
    for index in range(parts):
        wide = of_part(expand_weight, index)
        feeds.append(
            gather(
                [wide[:, c * D : (c + 1) * D] for c in range(tall)]
                + [shrink_weight[index * sub : (index + 1) * sub]]
            )
        )
    packed = lax.all_gather(gains_biases.astype(bf16), "seq", axis=0, tiled=True)
    vector = packed.astype(f32)
    gain_one = vector[0:D]
    shift_one = vector[D : 2 * D]
    gain_two = vector[2 * D : 3 * D]
    shift_two = vector[3 * D : 4 * D]
    bias_attend = vector[4 * D : 7 * D]
    bias_merge = vector[7 * D : 8 * D]
    bias_expand = vector[8 * D : 8 * D + FF]
    bias_shrink = vector[8 * D + FF :]

    bounds = jnp.cumsum(lengths[0])

    def label(place):
        return jnp.sum((bounds <= place[..., None]).astype(jnp.int32), -1)

    positions = device * rows + jnp.arange(rows, dtype=jnp.int32)
    segment = label(positions)
    starts = jnp.sum(jnp.where(bounds[None, :] <= positions[:, None], lengths[0][None, :], 0), -1)
    offset = positions - starts
    edges = device * rows + jnp.arange(count, dtype=jnp.int32) * CHUNK
    before = jnp.zeros((8,), jnp.int32).at[:count].set(label(edges - 1))
    final = jnp.zeros((8,), jnp.int32).at[:count].set(label(edges + CHUNK - 1))
    final = final.at[7].set(segment[-1])
    marks = jnp.broadcast_to(jnp.concatenate([before, final])[:, None], (16, LANES)).astype(f32)
    halfway = ROT // 2
    inverse = jnp.exp(jnp.arange(halfway, dtype=f32) * (-2.0 * math.log(BASE) / ROT))
    angles = offset.astype(f32)[:, None] * inverse
    cosine, sines = jnp.cos(angles), jnp.sin(angles)
    rest = jnp.ones((rows, HEAD - ROT), f32)
    none = jnp.zeros((rows, HEAD - ROT), f32)
    part = jnp.zeros((rows, halfway), f32)
    table = jnp.stack(
        [
            jnp.tile(jnp.concatenate([cosine, cosine, rest], 1), (1, 2)),
            jnp.tile(jnp.concatenate([-sines, part, none], 1), (1, 2)),
            jnp.tile(jnp.concatenate([part, sines, none], 1), (1, 2)),
            jnp.broadcast_to(segment.astype(f32)[:, None], (rows, 2 * HEAD)),
        ]
    )
    row_table = jnp.broadcast_to(segment.astype(f32)[None, :], (8, rows))
    const_np, weight_np = group_tables()
    const, weighting = jnp.asarray(const_np), jnp.asarray(weight_np)

    inputs = tokens[0].astype(f32)
    normed, root = layer_parts(inputs)
    low_one = (normed * gain_one + shift_one).astype(bf16)
    low_two = (normed * gain_two + shift_two).astype(bf16)

    flipped_one = lax.optimization_barrier(low_one.T)
    flipped_two = lax.optimization_barrier(low_two.T)

    def feed(index, done, parted):
        width = 2 * sub
        per = D // width
        held = (n // 2 if parted else n, 2 * tall, own, D)
        many = 2 if parted else 1
        return pl.pallas_call(
            feed_kernel,
            grid=(n // 2,),
            in_specs=[
                whole((rows, D)),
                whole((D, rows)),
                whole((rows, D)),
                pl.BlockSpec((n, 1, own, width), lambda g: (0, g // per, 0, g % per)),
                pl.BlockSpec((2, tall, own, D), lambda g: (g, 1, 0, 0)),
                pl.BlockSpec((1, width), lambda g: (0, g)),
                scalar(),
                pl.BlockSpec(memory_space=pl.ANY),
            ],
            out_specs=[
                total_of((rows, D)),
                total_of((rows, D)),
                pl.BlockSpec((8, width), lambda g: (0, g)),
                *[total_of(held)] * many,
            ],
            out_shape=[
                shaped((rows, D), f32),
                shaped((rows, D), f32),
                shaped((8, FF // parts), f32),
                *[shaped(held, bf16)] * many,
            ],
            compiler_params=params(),
            cost_estimate=pl.CostEstimate(
                flops=24 * rows * D * FF // parts,
                bytes_accessed=10 * D * FF // parts,
                transcendentals=rows * FF // parts,
            ),
            name="feed",
        )(
            low_two, flipped_two, grad_out, feeds[index], feeds[index],
            of_part(bias_expand[None, :], index), core_ref, done,
        )

    def projection(index):
        return pl.BlockSpec((n, 1, own, LANES), lambda g: (0, index, 0, g))

    constants = [whole((3, LANES, LANES)), whole((1, LANES))]
    tables = [whole((4, rows, 2 * HEAD)), whole((16, LANES))]
    query, key, value, value_low, turned_query, turned_key, summary = pl.pallas_call(
        qkv_kernel,
        grid=(NGROUP,),
        in_specs=[
            whole((rows, D)),
            *[projection(index) for index in range(3)],
            columns(3),
            *tables,
            *constants,
        ],
        out_specs=[columns(rows)] * 6 + [columns(STATE)],
        out_shape=[shaped((rows, D), bf16)] * 6 + [shaped((STATE, D), f32)],
        compiler_params=params(),
        cost_estimate=pl.CostEstimate(
            flops=6 * rows * D * D + 22 * rows * D * LANES,
            bytes_accessed=20 * rows * D,
            transcendentals=2 * rows * D,
        ),
        name="qkv",
    )(low_one, attend, attend, attend, bias_attend.reshape(3, D), table, marks, const, weighting)

    reaches = range(1, n // 2 + 1)
    own_before, own_final = label(device * rows - 1), segment[-1]
    carried = jnp.zeros_like(summary)
    for far in reaches:
        came = lax.ppermute(summary, "seq", [(e, e + far) for e in range(n - far)])
        same = (device >= far) & (label((device - far + 1) * rows - 1) == own_before)
        carried = carried + jnp.where(same, came, 0.0)

    _, grad_query, part_key, part_value, grad_carried, query_bias, attend_out, send, keep = pl.pallas_call(
        attend_kernel,
        grid=(NGROUP,),
        in_specs=[
            *[columns(rows)] * 5,
            columns(STATE),
            whole((rows, D)),
            pl.BlockSpec((LANES // own, 1, own, D), lambda g: (g, 3, 0, 0)),
            whole((4, rows, 2 * HEAD)),
            whole((8, rows)),
            whole((16, LANES)),
            whole((3, LANES, LANES)),
            scalar(),
        ],
        out_specs=[columns(rows)] * 4
        + [columns(STATE), columns(8), total_of((rows, D))]
        + [pl.BlockSpec((LANES // own // 2, 1, own, D), lambda g: (g, 3, 0, 0))] * 2,
        out_shape=[
            shaped((rows, D), bf16),
            shaped((rows, D), bf16),
            shaped((rows, D), f32),
            shaped((rows, D), f32),
            shaped((STATE, D), f32),
            shaped((8, D), f32),
            shaped((rows, D), f32),
            shaped((n // 2, 4, own, D), f32),
            shaped((n // 2, 4, own, D), f32),
        ],
        scratch_shapes=[pltpu.VMEM((rows, LANES), kind) for kind in (bf16, bf16, f32)],
        compiler_params=params(),
        cost_estimate=pl.CostEstimate(
            flops=2 * rows * D * D + 150 * rows * D * LANES,
            bytes_accessed=24 * rows * D,
            transcendentals=0,
        ),
        name="attend",
    )(
        query, key, value, value_low, turned_query, carried,
        grad_out, attend, table, row_table, marks, const, core_ref,
    )

    fed = [feed(0, grad_carried, False)]

    returned = jnp.zeros_like(summary)
    for far in reaches:
        came = lax.ppermute(grad_carried, "seq", [(e + far, e) for e in range(n - far)])
        same = (device + far < n) & (label((device + far) * rows - 1) == own_final)
        returned = returned + jnp.where(same, came, 0.0)

    sides = pl.BlockSpec((n // 2, 3, own, LANES), lambda g: (0, 0, 0, g))
    rest_bias, grad_one, send, keep = pl.pallas_call(
        finish_kernel,
        grid=(NGROUP,),
        in_specs=[columns(rows)] * 7
        + [columns(STATE), *tables, whole((3, LANES, LANES))]
        + [projection(index) for index in range(3)]
        + [whole((D, rows)), scalar()]
        + [pl.BlockSpec(memory_space=pl.ANY)] * 3,
        out_specs=[columns(16), total_of((rows, D)), sides, sides],
        out_shape=[
            shaped((16, D), f32),
            shaped((rows, D), f32),
            shaped((n // 2, 4, own, D), f32),
            shaped((n // 2, 4, own, D), f32),
        ],
        input_output_aliases={16: 2, 17: 3},
        compiler_params=params(),
        cost_estimate=pl.CostEstimate(
            flops=12 * rows * D * D + 24 * rows * D * LANES,
            bytes_accessed=18 * rows * D,
            transcendentals=0,
        ),
        name="finish",
    )(
        key, value, value_low, turned_key, grad_query, part_key, part_value, returned,
        table, marks, const, attend, attend, attend, flipped_one, core_ref, send, keep, fed[0][2],
    )

    for index in range(1, parts):
        fed.append(feed(index, rest_bias, True))

    bits = n.bit_length() - 1

    def exchange(array, bit):
        return lax.ppermute(array, "seq", [(i, i ^ (1 << bit)) for i in range(n)])

    def scatter(send, keep):
        came = exchange(send, 0)
        middle = keep.shape[1] // 2
        order = list(range(1, bits))
        turned = (bits - 1) // 2
        orders = order, order[turned:] + order[:turned]
        places = order[::-1]
        deep = keep.reshape((2,) * (bits - 1) + keep.shape[1:])
        came = came.reshape(deep.shape)
        sides = [[(deep, places, side * middle), (came, places, side * middle)] for side in range(2)]

        def pick(terms, fixed):
            total = 0.0
            for array, axes, start in terms:
                starts = [fixed.get(bit, 0) for bit in axes] + [start, 0, 0]
                sizes = [1 if bit in fixed else 2 for bit in axes] + [middle, own, D]
                value = lax.dynamic_slice(array, starts, sizes).astype(f32)
                kept = [2 for bit in places if bit not in fixed]
                total = total + value.reshape(kept + [middle, own, D])
            return total

        for place in range(bits - 1):
            for side in range(2):
                bit, earlier = orders[side][place], orders[side][:place]
                fixed = {b: (device >> b) & 1 for b in earlier}
                fixed[bit] = 1 - ((device >> bit) & 1)
                other = pick(sides[side], fixed).astype(bf16)
                left = [b for b in places if b not in fixed]
                sides[side].append((exchange(other, bit), left, 0))
        fixed = {b: (device >> b) & 1 for b in order}
        return [pick(terms, fixed) for terms in sides]

    groups = lax.axis_size("dp")
    group = lax.axis_index("dp")

    def sum_groups(value, fine):
        blocks = value.shape[0]
        shares = value.reshape(blocks, groups, own // groups, D)
        rolls = {far: [(i, (i + far) % groups) for i in range(groups)] for far in range(1, groups)}

        def share(which):
            return lax.dynamic_index_in_dim(shares, which % groups, 1, False)

        total = share(group)
        for far, pairs in rolls.items():
            total = total + lax.ppermute(share(group + far).astype(bf16), "dp", pairs).astype(f32)
        high = lax.reduce_precision(total, 8, 7)
        total = jnp.concatenate([high, (total - high)[:fine]], 0).astype(bf16)
        result = jnp.zeros((blocks + fine,) + shares.shape[1:], bf16)
        result = lax.dynamic_update_index_in_dim(result, total, group, 1)
        for far, pairs in rolls.items():
            came = lax.ppermute(total, "dp", pairs)
            result = lax.dynamic_update_index_in_dim(result, came, (group - far) % groups, 1)
        return result.reshape(blocks + fine, own, D)

    def sum_all(value):
        for bit in range(bits):
            value = value + exchange(value, bit)
        for bit in range(groups.bit_length() - 1):
            pairs = [(i, i ^ (1 << bit)) for i in range(groups)]
            value = value + lax.ppermute(value, "dp", pairs)
        return value

    first_part = lax.psum_scatter(fed[0][3], "seq", scatter_dimension=0, tiled=False)
    feed_sums = [lax.psum([first_part[:tall], first_part[tall:]], "dp")]
    attend_sum = sum_groups(jnp.concatenate(scatter(send, keep), 0), 2)
    for index in range(1, parts):
        pieces = [piece.astype(bf16) for piece in scatter(*fed[index][3:])]
        feed_sums.append(lax.psum(pieces, "dp"))

    grad_float = grad_out.astype(f32)
    result = inputs + attend_out + bias_merge + bias_shrink + sum(f[0] for f in fed)
    block_output = result.astype(bf16)[None]
    grad_two = sum(f[1] for f in fed)
    grad_bias_out = jnp.sum(grad_float, 0)
    pulled = grad_one * gain_one + grad_two * gain_two
    drop = jnp.mean(pulled, -1, keepdims=True)
    lean = jnp.mean(pulled * normed, -1, keepdims=True)
    input_grad = (grad_float + root * (pulled - drop - normed * lean)).astype(bf16)[None]
    feed_bias = jnp.concatenate(
        [fed[p][2][0, j * sub : (j + 1) * sub] for j in range(n) for p in range(parts)]
    )
    grad_vector = jnp.concatenate(
        [
            jnp.sum(grad_one * normed, 0),
            jnp.sum(grad_one, 0),
            jnp.sum(grad_two * normed, 0),
            jnp.sum(grad_two, 0),
            query_bias[0],
            rest_bias[0],
            rest_bias[8],
            grad_bias_out,
            feed_bias,
            grad_bias_out,
        ]
    )
    vector_sum = sum_all(grad_vector.reshape(-1, 128)).reshape(-1)
    share = gains_biases.shape[0]
    own_vector = lax.dynamic_slice(vector_sum, (device * share,), (share,))

    strips = 8

    wide_cols = FF // parts // strips
    per = D // wide_cols
    held = None
    expand_sums, shrink_sums = [], []
    for index in range(parts):
        of_expand = pl.BlockSpec((own, wide_cols), lambda g: (0, g * parts + index))
        of_shrink = pl.BlockSpec((sub // strips, D), lambda g: (index * strips + g, 0))
        before_specs = [] if held is None else [pl.BlockSpec(memory_space=pl.ANY)] * 6
        expand_norm, shrink_norm, *held = pl.pallas_call(
            lamb_feed_kernel,
            grid=(strips,),
            in_specs=[of_expand] * 3
            + [pl.BlockSpec((1, own, wide_cols), lambda g: (g // per, 0, g % per))]
            + [of_shrink] * 3
            + [pl.BlockSpec((sub // strips, D), lambda g: (g, 0))]
            + before_specs,
            out_specs=[total_of((2, 8, wide_cols)), total_of((2, 8, D))]
            + [of_expand] * 3
            + [of_shrink] * 3,
            out_shape=[shaped((2, 8, wide_cols), f32), shaped((2, 8, D), f32)]
            + [shaped((own, FF), f32)] * 3
            + [shaped((FF // n, D), f32)] * 3,
            input_output_aliases={} if held is None else {8 + i: 2 + i for i in range(6)},
            compiler_params=params(),
            name="lamb_feed",
        )(
            expand_weight, expand_first, expand_second, feed_sums[index][0],
            shrink_weight, shrink_first, shrink_second, flat(feed_sums[index][1]),
            *([] if held is None else held),
        )
        expand_sums.append(jnp.sum(expand_norm, (1, 2)))
        shrink_sums.append(jnp.sum(shrink_norm, (1, 2)))
    expand_mean, expand_square, expand_update, shrink_mean, shrink_square, shrink_update = held
    block_of = pl.BlockSpec((own, D), lambda g: (0, g))
    attend_norm, merge_norm, *held = pl.pallas_call(
        lamb_attend_kernel,
        grid=(3,),
        in_specs=[block_of] * 3 + [whole((own, D))] * 3 + [whole((6, own, D))],
        out_specs=[total_of((2, 8, D))] * 2 + [block_of] * 3 + [total_of((own, D))] * 3,
        out_shape=[shaped((2, 8, D), f32)] * 2
        + [shaped((own, 3 * D), f32)] * 3
        + [shaped((own, D), f32)] * 3,
        compiler_params=params(),
        name="lamb_attend",
    )(
        attend_weight, attend_first, attend_second, merge_weight, merge_first, merge_second,
        attend_sum,
    )
    attend_mean, attend_square, attend_update, merge_mean, merge_square, merge_update = held
    vector_mean, vector_square, vector_update = lamb_update(
        gains_biases, vector_first, vector_second, own_vector, 0.0
    )
    local = jnp.concatenate(
        [
            jnp.sum(attend_norm, (1, 2)),
            jnp.sum(merge_norm, (1, 2)),
            sum(expand_sums),
            sum(shrink_sums),
            jnp.stack([jnp.sum(gains_biases * gains_biases), jnp.sum(vector_update * vector_update)]),
        ]
    )
    squares = lax.psum(local, "seq")
    fresh = pl.pallas_call(
        renew_kernel,
        grid=(strips,),
        in_specs=[scalar()]
        + [pl.BlockSpec((own, 3 * D // strips), lambda g: (0, g))] * 2
        + [pl.BlockSpec((own, D // strips), lambda g: (0, g))] * 2
        + [pl.BlockSpec((own, FF // strips), lambda g: (0, g))] * 2
        + [pl.BlockSpec((FF // n // strips, D), lambda g: (g, 0))] * 2,
        out_specs=[
            pl.BlockSpec((own, 3 * D // strips), lambda g: (0, g)),
            pl.BlockSpec((own, D // strips), lambda g: (0, g)),
            pl.BlockSpec((own, FF // strips), lambda g: (0, g)),
            pl.BlockSpec((FF // n // strips, D), lambda g: (g, 0)),
        ],
        out_shape=[
            shaped((own, 3 * D), f32),
            shaped((own, D), f32),
            shaped((own, FF), f32),
            shaped((FF // n, D), f32),
        ],
        compiler_params=params(),
        name="renew",
    )(
        squares, attend_weight, attend_update, merge_weight, merge_update,
        expand_weight, expand_update, shrink_weight, shrink_update,
    )
    roots = jnp.sqrt(squares.reshape(5, 2).T.reshape(10))
    vector_fresh = gains_biases - RATE * (roots[4] / (roots[9] + EPSILON)) * vector_update
    return (
        block_output, input_grad,
        fresh[0], attend_mean, attend_square,
        fresh[1], merge_mean, merge_square,
        fresh[2], expand_mean, expand_square,
        fresh[3], shrink_mean, shrink_square,
        vector_fresh, vector_mean, vector_square,
        roots,
    )


def solution(mesh):
    matrix, line = P("seq", None), P("seq")
    stream = P("dp", "seq", None)
    return jax.shard_map(
        per_device,
        mesh=mesh,
        in_specs=(stream, stream, P("dp", None))
        + (matrix,) * 4
        + (line,)
        + (matrix,) * 8
        + (line,) * 2,
        out_specs=(stream, stream) + (matrix,) * 12 + (line,) * 3 + (P(),),
        check_vma=False,
    )
```

```python
import math

import jax
import jax.numpy as jnp
import ml_dtypes
import numpy as np
from jax import lax
from jax.experimental import pallas as pl
from jax.experimental.pallas import tpu as pltpu
from jax.sharding import PartitionSpec as P

D = 1024
FF = 4096
H = 16
HEAD = 64
ROT = 16
FEAT = 64
STEP = 10

SCALE = 0.25
BASE = 10000.0
BETA_ONE = 0.9
BETA_TWO = 0.999
EPSILON = 1e-06
DECAY = 0.01
RATE = 0.25

CHUNK = 256
LANES = 256
EACH = LANES // HEAD
NGROUP = D // LANES
STATE = HEAD + 8
ROOM = 56 * 1024 * 1024
f32 = jnp.float32
bf16 = jnp.bfloat16


def feature_tables(head, feats):
    row_index = np.arange(head)[:, None]
    col_index = np.arange(head)[None, :]
    cosine = np.sqrt(2.0 / head) * np.cos(np.pi * (2 * col_index + 1) * row_index / (2.0 * head))
    cosine[0, :] = cosine[0, :] / np.sqrt(2.0)
    entry = np.arange(head)[:, None] + 1.0
    column = np.arange(feats)[None, :] + 0.5
    first_point = np.clip(np.mod(column / feats + entry * 0.7548776662, 1.0), 0.01, 0.99)
    second_point = np.mod(column * 0.569840291 + entry * 0.6180339887, 1.0)
    omega = np.sqrt(-2.0 * np.log(first_point)) * np.cos(2.0 * np.pi * second_point)
    matrix = cosine.T @ omega * SCALE
    weighting = (1.5 + np.cos(2.0 * np.pi * column[0] / feats)) / (1.5 * feats)
    return (matrix.astype(np.float32), weighting.astype(np.float32))


def group_tables():
    matrix, weighting = feature_tables(HEAD, FEAT)
    eye = np.eye(EACH, dtype=np.float32)
    wide = np.kron(eye, matrix)
    high = wide.astype(ml_dtypes.bfloat16)
    low = (wide - high.astype(np.float32)).astype(ml_dtypes.bfloat16)
    ones = np.kron(eye, np.ones((HEAD, HEAD), np.float32)).astype(ml_dtypes.bfloat16)
    return np.stack([high, low, ones]), np.tile(weighting, EACH)[None, :]


def dot_nn(a, b):
    return lax.dot_general(a, b, (((1,), (0,)), ((), ())), preferred_element_type=f32)


def dot_nt(a, b):
    return lax.dot_general(a, b, (((1,), (1,)), ((), ())), preferred_element_type=f32)


def dot_tn(a, b):
    return lax.dot_general(a, b, (((0,), (0,)), ((), ())), preferred_element_type=f32)


def halves(value):
    high = value.astype(bf16)
    return high, (value - high.astype(f32)).astype(bf16)


def dot_three(dot, high, low, other_high, other_low):
    return dot(high, other_high) + dot(low, other_high) + dot(high, other_low)


def twice(table):
    return jnp.concatenate([table, table], axis=1)


def flat(value):
    return value.reshape(-1, value.shape[-1])


def head_mask(index, dtype):
    lane = lax.broadcasted_iota(jnp.int32, (1, LANES), 1)
    inside = (lane >= index * HEAD) & (lane < (index + 1) * HEAD)
    return jnp.where(inside, 1.0, 0.0).astype(dtype)


def turn(value, table_ref):
    cosine, first, second = (twice(table_ref[i]) for i in range(3))
    half = ROT // 2
    return (
        value * cosine
        + pltpu.roll(value, LANES - half, 1) * first
        + pltpu.roll(value, half, 1) * second
    )


def turn_back(grad, table_ref):
    cosine, first, second = (twice(table_ref[i]) for i in range(3))
    half = ROT // 2
    return (
        grad * cosine
        + pltpu.roll(grad * first, half, 1)
        + pltpu.roll(grad * second, LANES - half, 1)
    )


def phi(value, const_ref, weight_ref):
    high, low = halves(value)
    project = (
        dot_nn(high, const_ref[0]) + dot_nn(low, const_ref[0]) + dot_nn(high, const_ref[1])
    )
    top, rest = halves(value * value)
    squares = dot_nn(top, const_ref[2]) + dot_nn(rest, const_ref[2])
    return weight_ref[...] * jnp.exp(project - (0.5 * SCALE * SCALE) * squares)


def phi_back(grad, feats, value, const_ref):
    high, low = halves(grad * feats)
    project = (
        dot_nt(high, const_ref[0]) + dot_nt(low, const_ref[0]) + dot_nt(high, const_ref[1])
    )
    total = dot_nn(high, const_ref[2]) + dot_nn(low, const_ref[2])
    return project - (SCALE * SCALE) * value * total


def spread(state_ref, const_ref):
    packed = state_ref[0:HEAD, :]
    tall = jnp.concatenate([packed] * EACH, axis=0)
    return tall * const_ref[2].astype(f32)


def squeeze_state(state):
    total = state[0:HEAD]
    for index in range(1, EACH):
        total = total + state[index * HEAD : (index + 1) * HEAD]
    return total


def key_kernel(
    h_ref, wk_ref, wv_ref, b_ref, table_ref, marks_ref, const_ref, weight_ref,
    k_ref, v_ref, vl_ref, uk_ref, s_ref,
):
    rows = h_ref[...]
    key = turn(dot_nn(rows, flat(wk_ref[...])) + b_ref[1:2, :], table_ref)
    uk_ref[...] = key.astype(bf16)
    feats = phi(key, const_ref, weight_ref).astype(bf16)
    k_ref[...] = feats
    value, value_low = halves(dot_nn(rows, flat(wv_ref[...])) + b_ref[2:3, :])
    v_ref[...] = value
    vl_ref[...] = value_low
    segment = twice(table_ref[3])
    tail = jnp.where(segment == marks_ref[15:16, :], 1.0, 0.0)
    kept = feats.astype(f32) * tail
    kept_low = kept.astype(bf16)
    state = (dot_tn(kept_low, value) + dot_tn(kept_low, value_low)) * const_ref[2].astype(f32)
    s_ref[0:HEAD, :] = squeeze_state(state)
    s_ref[HEAD:STATE, :] = jnp.broadcast_to(jnp.sum(kept, 0, keepdims=True), (8, LANES))


def query_kernel(
    h_ref, wq_ref, b_ref, table_ref, const_ref, weight_ref, done_ref, q_ref, uq_ref
):
    query = turn(dot_nn(h_ref[...], flat(wq_ref[...])) + b_ref[0:1, :], table_ref)
    uq_ref[...] = query.astype(bf16)
    q_ref[...] = phi(query, const_ref, weight_ref).astype(bf16)


def attend_kernel(
    q_ref, k_ref, v_ref, vl_ref, uq_ref, s_ref, g_ref, wm_ref, table_ref, row_ref, marks_ref, const_ref, core_ref, done_ref,
    mixed_ref, dq_ref, dk_ref, dv_ref, ds_ref, bias_ref, out_ref, send_ref, keep_ref,
    dnum_ref, dlow_ref, dden_ref,
):
    count = q_ref.shape[0] // CHUNK
    merge = flat(wm_ref[...])
    state = spread(s_ref, const_ref)
    total = s_ref[HEAD : HEAD + 1, :]
    blocks = const_ref[2].astype(f32)
    masks = [head_mask(index, bf16) for index in range(EACH)]
    lower = lax.broadcasted_iota(jnp.int32, (CHUNK, CHUNK), 0) >= lax.broadcasted_iota(
        jnp.int32, (CHUNK, CHUNK), 1
    )
    bias = jnp.zeros((1, LANES), f32)
    for c in range(count):
        here = pl.ds(c * CHUNK, CHUNK)
        query, key = q_ref[here, :], k_ref[here, :]
        value, value_low = v_ref[here, :], vl_ref[here, :]
        segment = twice(table_ref[3, here, :])
        before, final = marks_ref[c : c + 1, :], marks_ref[8 + c : 9 + c, :]
        reach = jnp.where(segment == before, 1.0, 0.0)
        tail = jnp.where(segment == final, 1.0, 0.0)
        keep = jnp.where(final == before, 1.0, 0.0)
        causal = lower & (segment == row_ref[0:1, c * CHUNK : (c + 1) * CHUNK])
        grad_mixed = dot_nt(g_ref[here, :], merge)
        state_high, state_low = halves(state)
        reached = query * reach.astype(bf16)
        number = dot_nn(reached, state_high) + dot_nn(reached, state_low)
        top, rest = halves(reached.astype(f32) * total)
        totals = dot_nn(top, const_ref[2]) + dot_nn(rest, const_ref[2])
        scores = []
        for index in range(EACH):
            mask = masks[index]
            score = jnp.where(causal, dot_nt(query, key * mask), 0.0)
            totals = totals + jnp.sum(score, 1, keepdims=True) * mask.astype(f32)
            high, low = halves(score)
            scores.append(high)
            number = number + dot_three(dot_nn, high, low, value * mask, value_low * mask)
        mixed = number / totals
        mixed_ref[here, :] = mixed.astype(bf16)
        slope_number = grad_mixed / totals
        dnum, dlow = halves(slope_number)
        dnum_ref[here, :] = dnum
        dlow_ref[here, :] = dlow
        top, rest = halves(slope_number * mixed)
        dden = -(dot_nn(top, const_ref[2]) + dot_nn(rest, const_ref[2]))
        dden_ref[here, :] = dden
        grad_query = reach * (
            dot_three(dot_nt, dnum, dlow, state_high, state_low) + dden * total
        )
        grad_key = jnp.zeros((CHUNK, LANES), f32)
        grad_value = jnp.zeros((CHUNK, LANES), f32)
        for index in range(EACH):
            mask = masks[index]
            column = dden[:, index * HEAD : index * HEAD + 1]
            slope = dot_three(dot_nt, dnum, dlow, value * mask, value_low * mask) + column
            high, low = halves(jnp.where(causal, slope, 0.0))
            grad_query = grad_query + dot_nn(high, key * mask) + dot_nn(low, key * mask)
            part_query = query * mask
            grad_key = grad_key + dot_tn(
                jnp.concatenate([high, low], 0), jnp.concatenate([part_query, part_query], 0)
            )
            both = dot_tn(scores[index], jnp.concatenate([dnum * mask, dlow * mask], 1))
            grad_value = grad_value + both[:, :LANES] + both[:, LANES:]
        dk_ref[here, :] = grad_key
        dv_ref[here, :] = grad_value
        grad = phi_back(grad_query, query.astype(f32), uq_ref[here, :].astype(f32), const_ref)
        grad = turn_back(grad, table_ref.at[:, here, :]).astype(bf16)
        dq_ref[here, :] = grad
        bias = bias + jnp.sum(grad.astype(f32), 0, keepdims=True)
        if c < count - 1:
            kept = key.astype(f32) * tail
            kept_low = kept.astype(bf16)
            state = keep * state + blocks * (dot_tn(kept_low, value) + dot_tn(kept_low, value_low))
            total = keep * total + jnp.sum(kept, 0, keepdims=True)
    bias_ref[...] = jnp.broadcast_to(bias, (8, LANES))
    grad_state = jnp.zeros((LANES, LANES), f32)
    grad_total = jnp.zeros((1, LANES), f32)
    for c in reversed(range(count)):
        here = pl.ds(c * CHUNK, CHUNK)
        segment = twice(table_ref[3, here, :])
        before, final = marks_ref[c : c + 1, :], marks_ref[8 + c : 9 + c, :]
        reach = jnp.where(segment == before, 1.0, 0.0)
        tail = jnp.where(segment == final, 1.0, 0.0)
        keep = jnp.where(final == before, 1.0, 0.0)
        if c < count - 1:
            high, low = halves(grad_state)
            dk_ref[here, :] += tail * (
                dot_three(dot_nt, v_ref[here, :], vl_ref[here, :], high, low) + grad_total
            )
            dv_ref[here, :] += tail * (dot_nn(k_ref[here, :], high) + dot_nn(k_ref[here, :], low))
        reached = q_ref[here, :].astype(f32) * reach
        low_reached = reached.astype(bf16)
        grad_state = keep * grad_state + blocks * (
            dot_tn(low_reached, dnum_ref[here, :]) + dot_tn(low_reached, dlow_ref[here, :])
        )
        grad_total = keep * grad_total + jnp.sum(reached * dden_ref[here, :], 0, keepdims=True)
    ds_ref[0:HEAD, :] = squeeze_state(grad_state)
    ds_ref[HEAD:STATE, :] = jnp.broadcast_to(grad_total, (8, LANES))
    mixed = mixed_ref[...]
    accumulate(out_ref, dot_nn(mixed, merge))
    part_owners(dot_tn(mixed, g_ref[...]), core_ref, send_ref, keep_ref)


def accumulate(ref, value):
    first = pl.program_id(0) == 0

    @pl.when(first)
    def _():
        ref[...] = value

    @pl.when(jnp.logical_not(first))
    def _():
        ref[...] += value


def part_owners(value, core_ref, send_ref, keep_ref):
    held = send_ref.shape
    pairs = value.reshape((held[0], 2) + held[1:]).astype(send_ref.dtype)
    even, odd = pairs[:, 0], pairs[:, 1]
    first = core_ref[0] == 0
    keep, send = jnp.where(first, even, odd), jnp.where(first, odd, even)
    keep_ref[...], send_ref[...] = keep, send


def finish_kernel(
    k_ref, v_ref, vl_ref, uk_ref, dq_ref, dk_ref, dv_ref, ds_ref, table_ref, marks_ref, const_ref,
    wq_ref, wk_ref, wv_ref, ht_ref, core_ref, sent_ref, kept_ref, done_ref,
    bias_ref, dh_ref, send_ref, keep_ref,
):
    segment = twice(table_ref[3])
    tail = jnp.where(segment == marks_ref[15:16, :], 1.0, 0.0)
    high, low = halves(spread(ds_ref, const_ref))
    key, value = k_ref[...], v_ref[...]
    grad_key = dk_ref[...] + tail * (
        dot_three(dot_nt, value, vl_ref[...], high, low) + ds_ref[HEAD : HEAD + 1, :]
    )
    grad_value = dv_ref[...] + tail * (dot_nn(key, high) + dot_nn(key, low))
    grad = phi_back(grad_key, key.astype(f32), uk_ref[...].astype(f32), const_ref)
    grad = turn_back(grad, table_ref).astype(bf16)
    low_value = grad_value.astype(bf16)
    bias_ref[0:8, :] = jnp.broadcast_to(jnp.sum(grad.astype(f32), 0, keepdims=True), (8, LANES))
    bias_ref[8:16, :] = jnp.broadcast_to(
        jnp.sum(low_value.astype(f32), 0, keepdims=True), (8, LANES)
    )
    grads = (dq_ref[...], grad, low_value)
    weights = (flat(wq_ref[...]), flat(wk_ref[...]), flat(wv_ref[...]))
    accumulate(dh_ref, sum(dot_nt(g, w) for g, w in zip(grads, weights)))
    first = core_ref[0] == 0
    for index, value in enumerate(grads):
        pairs = dot_nn(ht_ref[...], value).reshape(-1, 2, send_ref.shape[2], LANES)
        keep_ref[:, index] = jnp.where(first, pairs[:, 0], pairs[:, 1])
        send_ref[:, index] = jnp.where(first, pairs[:, 1], pairs[:, 0])


def normal_cdf(value):
    bell = jnp.exp(-0.5 * value * value)
    near = jnp.abs(value) * (0.3275911 * math.sqrt(0.5)) + 1.0
    guess = pl.reciprocal(near, approx=True)
    t = guess * (2.0 - near * guess)
    poly = 0.5 * 1.061405429
    for factor in (-1.453152027, 1.421413741, -0.284496736, 0.254829592):
        poly = poly * t + 0.5 * factor
    tail = poly * t * bell
    return jnp.where(value >= 0.0, 1.0 - tail, tail), bell


def feed_kernel(
    h_ref, ht_ref, g_ref, we_ref, ws_ref, be_ref, core_ref, done_ref,
    out_ref, dh_ref, bias_ref, *grad_refs,
):
    step = pl.program_id(0)
    grad_out, rows_in, flipped = g_ref[...], h_ref[...], ht_ref[...]
    expand, shrink = flat(we_ref[...]), flat(ws_ref[...])
    width = expand.shape[1]
    half = width // 2
    _, blocks, rows, _ = grad_refs[0].shape
    block = step // (D // width)
    first = core_ref[0] == 0

    def products(side):
        cut = slice(side * half, (side + 1) * half)
        pre = dot_nn(rows_in, expand[:, cut]) + be_ref[:, cut]
        return pre, dot_nt(grad_out, shrink[cut])

    def pointwise(side, pre, grad):
        cdf, bell = normal_cdf(pre)
        active = (pre * cdf).astype(bf16)
        slope = cdf + pre * bell * (1.0 / math.sqrt(2.0 * math.pi))
        grad = (grad * slope).astype(bf16)
        bias_ref[:, side * half : (side + 1) * half] = jnp.broadcast_to(
            jnp.sum(grad.astype(f32), 0, keepdims=True), (8, half)
        )
        return active, grad

    def gradients(side, active, grad):
        start = lax.rem(step, D // width) * width + side * half
        lanes = pl.ds(pl.multiple_of(start, half), half)
        wide = dot_nn(flipped, grad).astype(bf16)
        tall = dot_tn(active, grad_out).astype(bf16).reshape(blocks // 2, rows, D)
        if len(grad_refs) == 1:
            grad_refs[0][:, block, :, lanes] = wide.reshape(-1, rows, half)
            grad_refs[0][2 * step + side, blocks // 2 :] = tall
        else:
            send_ref, keep_ref = grad_refs
            pairs = wide.reshape(-1, 2, rows, half)
            keep_ref[:, block, :, lanes] = jnp.where(first, pairs[:, 0], pairs[:, 1])
            send_ref[:, block, :, lanes] = jnp.where(first, pairs[:, 1], pairs[:, 0])

            @pl.when(first == (side == 0))
            def _():
                keep_ref[step, blocks // 2 :] = tall

            @pl.when(first != (side == 0))
            def _():
                send_ref[step, blocks // 2 :] = tall

    left = products(0)
    left = pointwise(0, *left)
    right = products(1)
    gradients(0, *left)
    right = pointwise(1, *right)
    forward = dot_nn(left[0], shrink[:half])
    backward = dot_nt(left[1], expand[:, :half])
    gradients(1, *right)
    accumulate(out_ref, forward + dot_nn(right[0], shrink[half:]))
    accumulate(dh_ref, backward + dot_nt(right[1], expand[:, half:]))


def lamb_step(master, first, second, grad, mean_ref, square_ref, update_ref, norms_ref):
    first, second, update = lamb_update(master, first, second, grad, DECAY)
    mean_ref[...], square_ref[...], update_ref[...] = first, second, update
    for index, value in enumerate((master, update)):
        squares = jnp.sum((value * value).reshape(-1, 8, value.shape[-1]), 0)
        accumulate(norms_ref.at[index], squares)


def lamb_feed_kernel(
    ep_ref, em_ref, es_ref, eg_ref, sp_ref, sm_ref, ss_ref, sg_ref, *refs
):
    enorm_ref, snorm_ref, *outs = refs[-8:]
    lamb_step(ep_ref[...], em_ref[...], es_ref[...], eg_ref[0].astype(f32), *outs[:3], enorm_ref)
    lamb_step(sp_ref[...], sm_ref[...], ss_ref[...], sg_ref[...].astype(f32), *outs[3:], snorm_ref)


def lamb_attend_kernel(
    ap_ref, am_ref, as_ref, mp_ref, mm_ref, ms_ref, grad_ref,
    anorm_ref, mnorm_ref, *outs,
):
    step = pl.program_id(0)
    grad = grad_ref[step].astype(f32)
    grad = grad + jnp.where(step < 2, grad_ref[jnp.minimum(4 + step, 5)].astype(f32), 0.0)
    lamb_step(ap_ref[...], am_ref[...], as_ref[...], grad, *outs[:3], anorm_ref)

    @pl.when(step == 0)
    def _():
        grad = grad_ref[3].astype(f32)
        lamb_step(mp_ref[...], mm_ref[...], ms_ref[...], grad, *outs[3:], mnorm_ref)


def renew_kernel(squares_ref, *refs):
    count = len(refs) // 3
    for index in range(count):
        master_ref, update_ref, fresh_ref = refs[2 * index], refs[2 * index + 1], refs[2 * count + index]
        lanes = (1, master_ref.shape[-1])
        weight = jnp.sqrt(jnp.full(lanes, squares_ref[2 * index], f32))
        change = jnp.sqrt(jnp.full(lanes, squares_ref[2 * index + 1], f32))
        ratio = RATE * (weight / (change + EPSILON))
        fresh_ref[...] = master_ref[...] - ratio * update_ref[...]


def whole(shape):
    return pl.BlockSpec(shape, lambda g: (0,) * len(shape), pipeline_mode=pl.Buffered(1))


def total_of(shape):
    return pl.BlockSpec(shape, lambda g: (0,) * len(shape))


def scalar():
    return pl.BlockSpec(memory_space=pltpu.SMEM)


def columns(rows, width=LANES, offset=0):
    return pl.BlockSpec((rows, width), lambda g: (0, g + offset))


def shaped(shape, dtype):
    return jax.ShapeDtypeStruct(shape, dtype)


def params():
    return pltpu.CompilerParams(vmem_limit_bytes=ROOM, dimension_semantics=("arbitrary",))


def layer_parts(inputs):
    center = inputs - jnp.mean(inputs, -1, keepdims=True)
    spread_of = jnp.mean(center * center, -1, keepdims=True)
    root = lax.rsqrt(spread_of + 1e-05)
    return center * root, root


def lamb_update(master, first, second, grad, decay):
    first = BETA_ONE * first + (1.0 - BETA_ONE) * grad
    second = BETA_TWO * second + (1.0 - BETA_TWO) * grad * grad
    update = (
        first / (1.0 - BETA_ONE**STEP) / (jnp.sqrt(second / (1.0 - BETA_TWO**STEP)) + EPSILON)
        + decay * master
    )
    return (first, second, update)


def per_device(
    tokens,
    cotangent,
    lengths,
    attend_weight,
    merge_weight,
    expand_weight,
    shrink_weight,
    gains_biases,
    attend_first,
    attend_second,
    merge_first,
    merge_second,
    expand_first,
    expand_second,
    shrink_first,
    shrink_second,
    vector_first,
    vector_second,
):
    rows = tokens.shape[1]
    count = rows // CHUNK
    n = lax.axis_size("seq")
    device = lax.axis_index("seq")
    grad_out = cotangent[0]
    own = D // n
    parts = 2 if FF // n >= 256 else 1
    sub = FF // n // parts
    tall = FF // D // parts
    core = lax.rem(device, 2)
    core_ref = core[None].astype(jnp.int32)

    def gather(blocks):
        shard = jnp.concatenate([block.astype(bf16) for block in blocks], 0)
        full = lax.all_gather(shard, "seq", axis=0, tiled=False)
        return full.reshape(n, shard.shape[0] // own, own, D)

    def of_part(array, index):
        return jnp.concatenate(
            [array[:, (j * parts + index) * sub : (j * parts + index + 1) * sub] for j in range(n)], 1
        )

    attend = gather([attend_weight[:, :D], attend_weight[:, D : 2 * D], attend_weight[:, 2 * D :]])
    merge = gather([merge_weight])
    feeds = []
    for index in range(parts):
        wide = of_part(expand_weight, index)
        feeds.append(
            gather(
                [wide[:, c * D : (c + 1) * D] for c in range(tall)]
                + [shrink_weight[index * sub : (index + 1) * sub]]
            )
        )
    packed = lax.all_gather(gains_biases.astype(bf16), "seq", axis=0, tiled=True)
    vector = packed.astype(f32)
    gain_one = vector[0:D]
    shift_one = vector[D : 2 * D]
    gain_two = vector[2 * D : 3 * D]
    shift_two = vector[3 * D : 4 * D]
    bias_attend = vector[4 * D : 7 * D]
    bias_merge = vector[7 * D : 8 * D]
    bias_expand = vector[8 * D : 8 * D + FF]
    bias_shrink = vector[8 * D + FF :]

    bounds = jnp.cumsum(lengths[0])

    def label(place):
        return jnp.sum((bounds <= place[..., None]).astype(jnp.int32), -1)

    positions = device * rows + jnp.arange(rows, dtype=jnp.int32)
    segment = label(positions)
    starts = jnp.sum(jnp.where(bounds[None, :] <= positions[:, None], lengths[0][None, :], 0), -1)
    offset = positions - starts
    edges = device * rows + jnp.arange(count, dtype=jnp.int32) * CHUNK
    before = jnp.zeros((8,), jnp.int32).at[:count].set(label(edges - 1))
    final = jnp.zeros((8,), jnp.int32).at[:count].set(label(edges + CHUNK - 1))
    final = final.at[7].set(segment[-1])
    marks = jnp.broadcast_to(jnp.concatenate([before, final])[:, None], (16, LANES)).astype(f32)
    halfway = ROT // 2
    inverse = jnp.exp(jnp.arange(halfway, dtype=f32) * (-2.0 * math.log(BASE) / ROT))
    angles = offset.astype(f32)[:, None] * inverse
    cosine, sines = jnp.cos(angles), jnp.sin(angles)
    rest = jnp.ones((rows, HEAD - ROT), f32)
    none = jnp.zeros((rows, HEAD - ROT), f32)
    part = jnp.zeros((rows, halfway), f32)
    table = jnp.stack(
        [
            jnp.tile(jnp.concatenate([cosine, cosine, rest], 1), (1, 2)),
            jnp.tile(jnp.concatenate([-sines, part, none], 1), (1, 2)),
            jnp.tile(jnp.concatenate([part, sines, none], 1), (1, 2)),
            jnp.broadcast_to(segment.astype(f32)[:, None], (rows, 2 * HEAD)),
        ]
    )
    row_table = jnp.broadcast_to(segment.astype(f32)[None, :], (8, rows))
    const_np, weight_np = group_tables()
    const, weighting = jnp.asarray(const_np), jnp.asarray(weight_np)

    inputs = tokens[0].astype(f32)
    normed, root = layer_parts(inputs)
    low_one = (normed * gain_one + shift_one).astype(bf16)
    low_two = (normed * gain_two + shift_two).astype(bf16)

    flipped_one = lax.optimization_barrier(low_one.T)
    flipped_two = lax.optimization_barrier(low_two.T)

    def feed(index, done, parted):
        width = 2 * sub
        per = D // width
        held = (n // 2 if parted else n, 2 * tall, own, D)
        many = 2 if parted else 1
        return pl.pallas_call(
            feed_kernel,
            grid=(n // 2,),
            in_specs=[
                whole((rows, D)),
                whole((D, rows)),
                whole((rows, D)),
                pl.BlockSpec((n, 1, own, width), lambda g: (0, g // per, 0, g % per)),
                pl.BlockSpec((2, tall, own, D), lambda g: (g, 1, 0, 0)),
                pl.BlockSpec((1, width), lambda g: (0, g)),
                scalar(),
                pl.BlockSpec(memory_space=pl.ANY),
            ],
            out_specs=[
                total_of((rows, D)),
                total_of((rows, D)),
                pl.BlockSpec((8, width), lambda g: (0, g)),
                *[total_of(held)] * many,
            ],
            out_shape=[
                shaped((rows, D), f32),
                shaped((rows, D), f32),
                shaped((8, FF // parts), f32),
                *[shaped(held, bf16)] * many,
            ],
            compiler_params=params(),
            cost_estimate=pl.CostEstimate(
                flops=24 * rows * D * FF // parts,
                bytes_accessed=10 * D * FF // parts,
                transcendentals=rows * FF // parts,
            ),
            name="feed",
        )(
            low_two, flipped_two, grad_out, feeds[index], feeds[index],
            of_part(bias_expand[None, :], index), core_ref, done,
        )

    def projection(index):
        return pl.BlockSpec((n, 1, own, LANES), lambda g: (0, index, 0, g))

    constants = [whole((3, LANES, LANES)), whole((1, LANES))]
    tables = [whole((4, rows, 2 * HEAD)), whole((16, LANES))]
    biases = bias_attend.reshape(3, D)
    key, value, value_low, turned_key, summary = pl.pallas_call(
        key_kernel,
        grid=(NGROUP,),
        in_specs=[
            whole((rows, D)),
            *[projection(index) for index in range(1, 3)],
            columns(3),
            *tables,
            *constants,
        ],
        out_specs=[columns(rows)] * 4 + [columns(STATE)],
        out_shape=[shaped((rows, D), bf16)] * 4 + [shaped((STATE, D), f32)],
        compiler_params=params(),
        cost_estimate=pl.CostEstimate(
            flops=4 * rows * D * D + 14 * rows * D * LANES,
            bytes_accessed=14 * rows * D,
            transcendentals=rows * D,
        ),
        name="keys",
    )(low_one, attend, attend, biases, table, marks, const, weighting)
    query, turned_query = pl.pallas_call(
        query_kernel,
        grid=(NGROUP,),
        in_specs=[
            whole((rows, D)),
            projection(0),
            columns(3),
            tables[0],
            *constants,
            pl.BlockSpec(memory_space=pl.ANY),
        ],
        out_specs=[columns(rows)] * 2,
        out_shape=[shaped((rows, D), bf16)] * 2,
        compiler_params=params(),
        cost_estimate=pl.CostEstimate(
            flops=2 * rows * D * D + 8 * rows * D * LANES,
            bytes_accessed=8 * rows * D,
            transcendentals=rows * D,
        ),
        name="queries",
    )(low_one, attend, biases, table, const, weighting, summary)

    fed = [feed(0, query, False)]

    reaches = range(1, n // 2 + 1)
    own_before, own_final = label(device * rows - 1), segment[-1]
    carried = jnp.zeros_like(summary)
    for far in reaches:
        came = lax.ppermute(summary, "seq", [(e, e + far) for e in range(n - far)])
        same = (device >= far) & (label((device - far + 1) * rows - 1) == own_before)
        carried = carried + jnp.where(same, came, 0.0)

    _, grad_query, part_key, part_value, grad_carried, query_bias, attend_out, send, keep = pl.pallas_call(
        attend_kernel,
        grid=(NGROUP,),
        in_specs=[
            *[columns(rows)] * 5,
            columns(STATE),
            whole((rows, D)),
            pl.BlockSpec((LANES // own, 1, own, D), lambda g: (g, 0, 0, 0)),
            whole((4, rows, 2 * HEAD)),
            whole((8, rows)),
            whole((16, LANES)),
            whole((3, LANES, LANES)),
            scalar(),
            pl.BlockSpec(memory_space=pl.ANY),
        ],
        out_specs=[columns(rows)] * 4
        + [columns(STATE), columns(8), total_of((rows, D))]
        + [pl.BlockSpec((LANES // own // 2, 1, own, D), lambda g: (g, 3, 0, 0))] * 2,
        out_shape=[
            shaped((rows, D), bf16),
            shaped((rows, D), bf16),
            shaped((rows, D), f32),
            shaped((rows, D), f32),
            shaped((STATE, D), f32),
            shaped((8, D), f32),
            shaped((rows, D), f32),
            shaped((n // 2, 4, own, D), f32),
            shaped((n // 2, 4, own, D), f32),
        ],
        scratch_shapes=[pltpu.VMEM((rows, LANES), kind) for kind in (bf16, bf16, f32)],
        compiler_params=params(),
        cost_estimate=pl.CostEstimate(
            flops=2 * rows * D * D + 150 * rows * D * LANES,
            bytes_accessed=24 * rows * D,
            transcendentals=0,
        ),
        name="attend",
    )(
        query, key, value, value_low, turned_query, carried,
        grad_out, merge, table, row_table, marks, const, core_ref, fed[0][2],
    )

    for index in range(1, parts):
        fed.append(feed(index, grad_carried, True))

    returned = jnp.zeros_like(summary)
    for far in reaches:
        came = lax.ppermute(grad_carried, "seq", [(e + far, e) for e in range(n - far)])
        same = (device + far < n) & (label((device + far) * rows - 1) == own_final)
        returned = returned + jnp.where(same, came, 0.0)

    sides = pl.BlockSpec((n // 2, 3, own, LANES), lambda g: (0, 0, 0, g))
    rest_bias, grad_one, send, keep = pl.pallas_call(
        finish_kernel,
        grid=(NGROUP,),
        in_specs=[columns(rows)] * 7
        + [columns(STATE), *tables, whole((3, LANES, LANES))]
        + [projection(index) for index in range(3)]
        + [whole((D, rows)), scalar()]
        + [pl.BlockSpec(memory_space=pl.ANY)] * 3,
        out_specs=[columns(16), total_of((rows, D)), sides, sides],
        out_shape=[
            shaped((16, D), f32),
            shaped((rows, D), f32),
            shaped((n // 2, 4, own, D), f32),
            shaped((n // 2, 4, own, D), f32),
        ],
        input_output_aliases={16: 2, 17: 3},
        compiler_params=params(),
        cost_estimate=pl.CostEstimate(
            flops=12 * rows * D * D + 24 * rows * D * LANES,
            bytes_accessed=18 * rows * D,
            transcendentals=0,
        ),
        name="finish",
    )(
        key, value, value_low, turned_key, grad_query, part_key, part_value, returned,
        table, marks, const, attend, attend, attend, flipped_one, core_ref, send, keep, fed[-1][2],
    )

    bits = n.bit_length() - 1

    def exchange(array, bit):
        return lax.ppermute(array, "seq", [(i, i ^ (1 << bit)) for i in range(n)])

    def scatter(keep, came):
        middle = keep.shape[1] // 2
        order = list(range(1, bits))
        turned = (bits - 1) // 2
        orders = order, order[turned:] + order[:turned]
        places = order[::-1]
        deep = keep.reshape((2,) * (bits - 1) + keep.shape[1:])
        came = came.reshape(deep.shape)
        sides = [[(deep, places, side * middle), (came, places, side * middle)] for side in range(2)]

        def pick(terms, fixed):
            total = 0.0
            for array, axes, start in terms:
                starts = [fixed.get(bit, 0) for bit in axes] + [start, 0, 0]
                sizes = [1 if bit in fixed else 2 for bit in axes] + [middle, own, D]
                value = lax.dynamic_slice(array, starts, sizes).astype(f32)
                kept = [2 for bit in places if bit not in fixed]
                total = total + value.reshape(kept + [middle, own, D])
            return total

        for place in range(bits - 1):
            for side in range(2):
                bit, earlier = orders[side][place], orders[side][:place]
                fixed = {b: (device >> b) & 1 for b in earlier}
                fixed[bit] = 1 - ((device >> bit) & 1)
                other = pick(sides[side], fixed).astype(bf16)
                left = [b for b in places if b not in fixed]
                sides[side].append((exchange(other, bit), left, 0))
        fixed = {b: (device >> b) & 1 for b in order}
        return jnp.concatenate([pick(terms, fixed) for terms in sides], 0)

    spot = jnp.stack([(device >> 1) & 1, (device >> 2) & 1]).astype(jnp.int32)

    def add_step(terms, outs, done, count):
        flat_terms = [term for group in terms for term in group]
        sizes = [len(group) for group in terms]

        def kernel(spot_ref, *refs):
            ins, out_refs = refs[: len(flat_terms)], refs[len(flat_terms) + len(done) :]
            at = 0
            for size, (out_ref, place) in zip(sizes, count(out_refs)):
                shape = out_ref.at[place].shape
                total = ins[at][...].astype(f32).reshape(shape)
                for ref in ins[at + 1 : at + size]:
                    total = total + ref[...].astype(f32).reshape(shape)
                out_ref[place] = total.astype(out_ref.dtype)
                at += size

        return pl.pallas_call(
            kernel,
            grid_spec=pltpu.PrefetchScalarGridSpec(
                num_scalar_prefetch=1,
                grid=(2,),
                in_specs=[spec for _, spec in flat_terms]
                + [pl.BlockSpec(memory_space=pl.ANY)] * len(done),
                out_specs=[spec for _, spec in outs],
            ),
            out_shape=[shape for shape, _ in outs],
            compiler_params=params(),
            name="add",
        )(spot, *[array for array, _ in flat_terms], *done)

    one, two = (1, 1, 1, own, D), (1, 1, 2, own, D)

    def step_one(keep, came, done):
        wide = pl.BlockSpec(two, lambda g, at: (g, 1 - at[0], 0, 0, 0))
        tall_part = pl.BlockSpec(two, lambda g, at: (1 - at[1], g, 1, 0, 0))
        out = shaped((2, 2, own, D), bf16), pl.BlockSpec((1, 2, own, D), lambda g, at: (g, 0, 0, 0))
        terms = [[(keep, wide), (came, wide)], [(keep, tall_part), (came, tall_part)]]
        first, second = add_step(terms, [out] * 2, done, lambda refs: [(ref, ...) for ref in refs])
        return first, exchange(first, 1), exchange(second, 2)

    def step_two(keep, came, first, second, done):
        wide = pl.BlockSpec(one, lambda g, at: (1 - at[1], at[0], g, 0, 0))
        tall_part = pl.BlockSpec(one, lambda g, at: (at[1], 1 - at[0], 2 + g, 0, 0))
        first_of = pl.BlockSpec((1, 1, own, D), lambda g, at: (1 - at[1], g, 0, 0))
        second_of = pl.BlockSpec((1, 1, own, D), lambda g, at: (1 - at[0], g, 0, 0))
        out = shaped((2, own, D), bf16), pl.BlockSpec((1, own, D), lambda g, at: (g, 0, 0))
        terms = [
            [(keep, wide), (came, wide), (first, first_of)],
            [(keep, tall_part), (came, tall_part), (second, second_of)],
        ]
        sent = add_step(terms, [out] * 2, done, lambda refs: [(ref, ...) for ref in refs])
        return exchange(sent[0], 2), exchange(sent[1], 1)

    def step_three(keep, came, first, second, last_first, last_second, kind, done):
        wide = pl.BlockSpec(one, lambda g, at: (at[1], at[0], g, 0, 0))
        tall_part = pl.BlockSpec(one, lambda g, at: (at[1], at[0], 2 + g, 0, 0))
        first_of = pl.BlockSpec((1, 1, own, D), lambda g, at: (at[1], g, 0, 0))
        second_of = pl.BlockSpec((1, 1, own, D), lambda g, at: (at[0], g, 0, 0))
        last = pl.BlockSpec((1, own, D), lambda g, at: (g, 0, 0))
        out = shaped((2, 2, own, D), kind), pl.BlockSpec((2, 1, own, D), lambda g, at: (0, g, 0, 0))
        terms = [
            [(keep, wide), (came, wide), (first, first_of), (last_first, last)],
            [(keep, tall_part), (came, tall_part), (second, second_of), (last_second, last)],
        ]
        result = add_step(terms, [out], done, lambda refs: [(refs[0], 0), (refs[0], 1)])
        return result[0].reshape(4, own, D)

    groups = lax.axis_size("dp")
    group = lax.axis_index("dp")

    def sum_groups(value, fine):
        blocks = value.shape[0]
        shares = value.reshape(blocks, groups, own // groups, D)
        rolls = {far: [(i, (i + far) % groups) for i in range(groups)] for far in range(1, groups)}

        def share(which):
            return lax.dynamic_index_in_dim(shares, which % groups, 1, False)

        total = share(group)
        for far, pairs in rolls.items():
            total = total + lax.ppermute(share(group + far).astype(bf16), "dp", pairs).astype(f32)
        high = lax.reduce_precision(total, 8, 7)
        total = jnp.concatenate([high, (total - high)[:fine]], 0).astype(bf16)
        result = jnp.zeros((blocks + fine,) + shares.shape[1:], bf16)
        result = lax.dynamic_update_index_in_dim(result, total, group, 1)
        for far, pairs in rolls.items():
            came = lax.ppermute(total, "dp", pairs)
            result = lax.dynamic_update_index_in_dim(result, came, (group - far) % groups, 1)
        return result.reshape(blocks + fine, own, D)

    def sum_all(value):
        for bit in range(bits):
            value = value + exchange(value, bit)
        for bit in range(groups.bit_length() - 1):
            pairs = [(i, i ^ (1 << bit)) for i in range(groups)]
            value = value + lax.ppermute(value, "dp", pairs)
        return value

    first_part = lax.psum_scatter(fed[0][3], "seq", scatter_dimension=0, tiled=False)
    feed_sums = [lax.psum(first_part, "dp")]
    if bits == 3 and parts == 2:
        deep = (2, 2, 4, own, D)
        feed_send, feed_keep = (array.reshape(deep) for array in fed[1][3:])
        feed_came = exchange(feed_send, 0)
        send, keep = send.reshape(deep), keep.reshape(deep)
        came = exchange(send, 0)
        begun, *feed_first = step_one(feed_keep, feed_came, [rest_bias])
        started, *first = step_one(keep, came, [begun, first_part])
        feed_second = step_two(feed_keep, feed_came, *feed_first, [started])
        second = step_two(keep, came, *first, feed_second)
        attend_part = step_three(keep, came, *first, *second, f32, [])
        feed_part = step_three(
            feed_keep, feed_came, *feed_first, *feed_second, bf16, [attend_part, feed_sums[0]]
        )
        feed_sums.append(lax.psum(feed_part, "dp"))
        grad_one = grad_one + 0.0 * started[0, 0, 0, 0].astype(f32)
    else:
        for index in range(1, parts):
            part = scatter(fed[index][4], exchange(fed[index][3], 0))
            feed_sums.append(lax.psum(part.astype(bf16), "dp"))
        attend_part = scatter(keep, exchange(send, 0))
    attend_sum = sum_groups(attend_part, 2)

    grad_float = grad_out.astype(f32)
    result = inputs + attend_out + bias_merge + bias_shrink + sum(f[0] for f in fed)
    block_output = result.astype(bf16)[None]
    grad_two = sum(f[1] for f in fed)
    grad_bias_out = jnp.sum(grad_float, 0)
    pulled = grad_one * gain_one + grad_two * gain_two
    drop = jnp.mean(pulled, -1, keepdims=True)
    lean = jnp.mean(pulled * normed, -1, keepdims=True)
    input_grad = (grad_float + root * (pulled - drop - normed * lean)).astype(bf16)[None]
    feed_bias = jnp.concatenate(
        [fed[p][2][0, j * sub : (j + 1) * sub] for j in range(n) for p in range(parts)]
    )
    grad_vector = jnp.concatenate(
        [
            jnp.sum(grad_one * normed, 0),
            jnp.sum(grad_one, 0),
            jnp.sum(grad_two * normed, 0),
            jnp.sum(grad_two, 0),
            query_bias[0],
            rest_bias[0],
            rest_bias[8],
            grad_bias_out,
            feed_bias,
            grad_bias_out,
        ]
    )
    grad_vector = grad_vector + 0.0 * attend_part[0, 0, 0].astype(f32)
    vector_sum = sum_all(grad_vector.reshape(-1, 128)).reshape(-1)
    share = gains_biases.shape[0]
    own_vector = lax.dynamic_slice(vector_sum, (device * share,), (share,))

    strips = 8

    wide_cols = FF // parts // strips
    per = D // wide_cols
    held = None
    expand_sums, shrink_sums = [], []
    for index in range(parts):
        of_expand = pl.BlockSpec((own, wide_cols), lambda g: (0, g * parts + index))
        of_shrink = pl.BlockSpec((sub // strips, D), lambda g: (index * strips + g, 0))
        before_specs = [] if held is None else [pl.BlockSpec(memory_space=pl.ANY)] * 6
        expand_norm, shrink_norm, *held = pl.pallas_call(
            lamb_feed_kernel,
            grid=(strips,),
            in_specs=[of_expand] * 3
            + [pl.BlockSpec((1, own, wide_cols), lambda g: (g // per, 0, g % per))]
            + [of_shrink] * 3
            + [pl.BlockSpec((sub // strips, D), lambda g: (strips + g, 0))]
            + before_specs,
            out_specs=[total_of((2, 8, wide_cols)), total_of((2, 8, D))]
            + [of_expand] * 3
            + [of_shrink] * 3,
            out_shape=[shaped((2, 8, wide_cols), f32), shaped((2, 8, D), f32)]
            + [shaped((own, FF), f32)] * 3
            + [shaped((FF // n, D), f32)] * 3,
            input_output_aliases={} if held is None else {8 + i: 2 + i for i in range(6)},
            compiler_params=params(),
            name="lamb_feed",
        )(
            expand_weight, expand_first, expand_second, feed_sums[index],
            shrink_weight, shrink_first, shrink_second, flat(feed_sums[index]),
            *([] if held is None else held),
        )
        expand_sums.append(jnp.sum(expand_norm, (1, 2)))
        shrink_sums.append(jnp.sum(shrink_norm, (1, 2)))
    expand_mean, expand_square, expand_update, shrink_mean, shrink_square, shrink_update = held
    block_of = pl.BlockSpec((own, D), lambda g: (0, g))
    attend_norm, merge_norm, *held = pl.pallas_call(
        lamb_attend_kernel,
        grid=(3,),
        in_specs=[block_of] * 3 + [whole((own, D))] * 3 + [whole((6, own, D))],
        out_specs=[total_of((2, 8, D))] * 2 + [block_of] * 3 + [total_of((own, D))] * 3,
        out_shape=[shaped((2, 8, D), f32)] * 2
        + [shaped((own, 3 * D), f32)] * 3
        + [shaped((own, D), f32)] * 3,
        compiler_params=params(),
        name="lamb_attend",
    )(
        attend_weight, attend_first, attend_second, merge_weight, merge_first, merge_second,
        attend_sum,
    )
    attend_mean, attend_square, attend_update, merge_mean, merge_square, merge_update = held
    vector_mean, vector_square, vector_update = lamb_update(
        gains_biases, vector_first, vector_second, own_vector, 0.0
    )
    local = jnp.concatenate(
        [
            jnp.sum(attend_norm, (1, 2)),
            jnp.sum(merge_norm, (1, 2)),
            sum(expand_sums),
            sum(shrink_sums),
            jnp.stack([jnp.sum(gains_biases * gains_biases), jnp.sum(vector_update * vector_update)]),
        ]
    )
    squares = lax.psum(local, "seq")
    fresh = pl.pallas_call(
        renew_kernel,
        grid=(4,),
        in_specs=[scalar()]
        + [pl.BlockSpec((own, 3 * D // 4), lambda g: (0, g))] * 2
        + [pl.BlockSpec((own, D // 4), lambda g: (0, g))] * 2
        + [pl.BlockSpec((own, FF // 4), lambda g: (0, g))] * 2
        + [pl.BlockSpec((FF // n // 4, D), lambda g: (g, 0))] * 2,
        out_specs=[
            pl.BlockSpec((own, 3 * D // 4), lambda g: (0, g)),
            pl.BlockSpec((own, D // 4), lambda g: (0, g)),
            pl.BlockSpec((own, FF // 4), lambda g: (0, g)),
            pl.BlockSpec((FF // n // 4, D), lambda g: (g, 0)),
        ],
        out_shape=[
            shaped((own, 3 * D), f32),
            shaped((own, D), f32),
            shaped((own, FF), f32),
            shaped((FF // n, D), f32),
        ],
        compiler_params=params(),
        name="renew",
    )(
        squares, attend_weight, attend_update, merge_weight, merge_update,
        expand_weight, expand_update, shrink_weight, shrink_update,
    )
    roots = jnp.sqrt(squares.reshape(5, 2).T.reshape(10))
    vector_fresh = gains_biases - RATE * (roots[4] / (roots[9] + EPSILON)) * vector_update
    return (
        block_output, input_grad,
        fresh[0], attend_mean, attend_square,
        fresh[1], merge_mean, merge_square,
        fresh[2], expand_mean, expand_square,
        fresh[3], shrink_mean, shrink_square,
        vector_fresh, vector_mean, vector_square,
        roots,
    )


def solution(mesh):
    matrix, line = P("seq", None), P("seq")
    stream = P("dp", "seq", None)
    return jax.shard_map(
        per_device,
        mesh=mesh,
        in_specs=(stream, stream, P("dp", None))
        + (matrix,) * 4
        + (line,)
        + (matrix,) * 8
        + (line,) * 2,
        out_specs=(stream, stream) + (matrix,) * 12 + (line,) * 3 + (P(),),
        check_vma=False,
    )
```

```python
import functools
import math

import jax
import jax.numpy as jnp
import ml_dtypes
import numpy as np
from jax import lax
from jax.experimental import pallas as pl
from jax.experimental.pallas import tpu as pltpu
from jax.sharding import PartitionSpec as P

D = 1024
FF = 4096
H = 16
HEAD = 64
ROT = 16
FEAT = 64
STEP = 10

SCALE = 0.25
BASE = 10000.0
BETA_ONE = 0.9
BETA_TWO = 0.999
EPSILON = 1e-06
DECAY = 0.01
RATE = 0.25

CHUNK = 256
LANES = 256
EACH = LANES // HEAD
NGROUP = D // LANES
STATE = HEAD + 8
ROOM = 56 * 1024 * 1024
f32 = jnp.float32
bf16 = jnp.bfloat16


def feature_tables(head, feats):
    row_index = np.arange(head)[:, None]
    col_index = np.arange(head)[None, :]
    cosine = np.sqrt(2.0 / head) * np.cos(np.pi * (2 * col_index + 1) * row_index / (2.0 * head))
    cosine[0, :] = cosine[0, :] / np.sqrt(2.0)
    entry = np.arange(head)[:, None] + 1.0
    column = np.arange(feats)[None, :] + 0.5
    first_point = np.clip(np.mod(column / feats + entry * 0.7548776662, 1.0), 0.01, 0.99)
    second_point = np.mod(column * 0.569840291 + entry * 0.6180339887, 1.0)
    omega = np.sqrt(-2.0 * np.log(first_point)) * np.cos(2.0 * np.pi * second_point)
    matrix = cosine.T @ omega * SCALE
    weighting = (1.5 + np.cos(2.0 * np.pi * column[0] / feats)) / (1.5 * feats)
    return (matrix.astype(np.float32), weighting.astype(np.float32))


def group_tables():
    matrix, weighting = feature_tables(HEAD, FEAT)
    eye = np.eye(EACH, dtype=np.float32)
    wide = np.kron(eye, matrix)
    high = wide.astype(ml_dtypes.bfloat16)
    low = (wide - high.astype(np.float32)).astype(ml_dtypes.bfloat16)
    ones = np.kron(eye, np.ones((HEAD, HEAD), np.float32)).astype(ml_dtypes.bfloat16)
    return np.stack([high, low, ones]), np.tile(weighting, EACH)[None, :]


def dot_nn(a, b):
    return lax.dot_general(a, b, (((1,), (0,)), ((), ())), preferred_element_type=f32)


def dot_nt(a, b):
    return lax.dot_general(a, b, (((1,), (1,)), ((), ())), preferred_element_type=f32)


def dot_tn(a, b):
    return lax.dot_general(a, b, (((0,), (0,)), ((), ())), preferred_element_type=f32)


def halves(value):
    high = value.astype(bf16)
    return high, (value - high.astype(f32)).astype(bf16)


def dot_three(dot, high, low, other_high, other_low):
    return dot(high, other_high) + dot(low, other_high) + dot(high, other_low)


def twice(table):
    return jnp.concatenate([table, table], axis=1)


def flat(value):
    return value.reshape(-1, value.shape[-1])


def head_mask(index, dtype):
    lane = lax.broadcasted_iota(jnp.int32, (1, LANES), 1)
    inside = (lane >= index * HEAD) & (lane < (index + 1) * HEAD)
    return jnp.where(inside, 1.0, 0.0).astype(dtype)


def turn(value, table_ref):
    cosine, first, second = (twice(table_ref[i]) for i in range(3))
    half = ROT // 2
    return (
        value * cosine
        + pltpu.roll(value, LANES - half, 1) * first
        + pltpu.roll(value, half, 1) * second
    )


def turn_back(grad, table_ref):
    cosine, first, second = (twice(table_ref[i]) for i in range(3))
    half = ROT // 2
    return (
        grad * cosine
        + pltpu.roll(grad * first, half, 1)
        + pltpu.roll(grad * second, LANES - half, 1)
    )


def phi(value, const_ref, weight_ref):
    high, low = halves(value)
    project = (
        dot_nn(high, const_ref[0]) + dot_nn(low, const_ref[0]) + dot_nn(high, const_ref[1])
    )
    top, rest = halves(value * value)
    squares = dot_nn(top, const_ref[2]) + dot_nn(rest, const_ref[2])
    return weight_ref[...] * jnp.exp(project - (0.5 * SCALE * SCALE) * squares)


def phi_back(grad, feats, value, const_ref):
    high, low = halves(grad * feats)
    project = (
        dot_nt(high, const_ref[0]) + dot_nt(low, const_ref[0]) + dot_nt(high, const_ref[1])
    )
    total = dot_nn(high, const_ref[2]) + dot_nn(low, const_ref[2])
    return project - (SCALE * SCALE) * value * total


def arrive(state_refs, weigh_ref):
    return sum(ref[...] * weigh_ref[i] for i, ref in enumerate(state_refs))


def spread(state, const_ref):
    packed = state[0:HEAD, :]
    tall = jnp.concatenate([packed] * EACH, axis=0)
    return tall * const_ref[2].astype(f32)


def squeeze_state(state):
    total = state[0:HEAD]
    for index in range(1, EACH):
        total = total + state[index * HEAD : (index + 1) * HEAD]
    return total


def key_kernel(
    h_ref, wk_ref, wv_ref, b_ref, table_ref, marks_ref, const_ref, weight_ref,
    k_ref, v_ref, vl_ref, uk_ref, s_ref,
):
    rows = h_ref[...]
    key = turn(dot_nn(rows, flat(wk_ref[...])) + b_ref[1:2, :], table_ref)
    uk_ref[...] = key.astype(bf16)
    feats = phi(key, const_ref, weight_ref).astype(bf16)
    k_ref[...] = feats
    value, value_low = halves(dot_nn(rows, flat(wv_ref[...])) + b_ref[2:3, :])
    v_ref[...] = value
    vl_ref[...] = value_low
    segment = twice(table_ref[3])
    tail = jnp.where(segment == marks_ref[15:16, :], 1.0, 0.0)
    kept = feats.astype(f32) * tail
    kept_low = kept.astype(bf16)
    state = (dot_tn(kept_low, value) + dot_tn(kept_low, value_low)) * const_ref[2].astype(f32)
    s_ref[0:HEAD, :] = squeeze_state(state)
    s_ref[HEAD:STATE, :] = jnp.broadcast_to(jnp.sum(kept, 0, keepdims=True), (8, LANES))


def query_kernel(
    h_ref, wq_ref, b_ref, table_ref, const_ref, weight_ref, done_ref, q_ref, uq_ref
):
    query = turn(dot_nn(h_ref[...], flat(wq_ref[...])) + b_ref[0:1, :], table_ref)
    uq_ref[...] = query.astype(bf16)
    q_ref[...] = phi(query, const_ref, weight_ref).astype(bf16)


def attend_kernel(far, *refs):
    state_refs, refs = refs[:far], refs[far:]
    (
        q_ref, k_ref, v_ref, vl_ref, uq_ref, weigh_ref, g_ref, wm_ref, table_ref, row_ref,
        marks_ref, const_ref, core_ref,
        dq_ref, dk_ref, dv_ref, ds_ref, bias_ref, out_ref, send_ref, keep_ref,
        mixed_ref, dnum_ref, dlow_ref, dden_ref,
    ) = refs
    came = arrive(state_refs, weigh_ref)
    count = q_ref.shape[0] // CHUNK
    merge = flat(wm_ref[...])
    state = spread(came, const_ref)
    total = came[HEAD : HEAD + 1, :]
    blocks = const_ref[2].astype(f32)
    masks = [head_mask(index, bf16) for index in range(EACH)]
    lower = lax.broadcasted_iota(jnp.int32, (CHUNK, CHUNK), 0) >= lax.broadcasted_iota(
        jnp.int32, (CHUNK, CHUNK), 1
    )
    bias = jnp.zeros((1, LANES), f32)
    for c in range(count):
        here = pl.ds(c * CHUNK, CHUNK)
        query, key = q_ref[here, :], k_ref[here, :]
        value, value_low = v_ref[here, :], vl_ref[here, :]
        segment = twice(table_ref[3, here, :])
        before, final = marks_ref[c : c + 1, :], marks_ref[8 + c : 9 + c, :]
        reach = jnp.where(segment == before, 1.0, 0.0)
        tail = jnp.where(segment == final, 1.0, 0.0)
        keep = jnp.where(final == before, 1.0, 0.0)
        causal = lower & (segment == row_ref[0:1, c * CHUNK : (c + 1) * CHUNK])
        grad_mixed = dot_nt(g_ref[here, :], merge)
        state_high, state_low = halves(state)
        reached = query * reach.astype(bf16)
        number = dot_nn(reached, state_high) + dot_nn(reached, state_low)
        top, rest = halves(reached.astype(f32) * total)
        totals = dot_nn(top, const_ref[2]) + dot_nn(rest, const_ref[2])
        scores = []
        for index in range(EACH):
            mask = masks[index]
            score = jnp.where(causal, dot_nt(query, key * mask), 0.0)
            totals = totals + jnp.sum(score, 1, keepdims=True) * mask.astype(f32)
            high, low = halves(score)
            scores.append(high)
            number = number + dot_three(dot_nn, high, low, value * mask, value_low * mask)
        mixed = number / totals
        mixed_ref[here, :] = mixed.astype(bf16)
        slope_number = grad_mixed / totals
        dnum, dlow = halves(slope_number)
        dnum_ref[here, :] = dnum
        dlow_ref[here, :] = dlow
        top, rest = halves(slope_number * mixed)
        dden = -(dot_nn(top, const_ref[2]) + dot_nn(rest, const_ref[2]))
        dden_ref[here, :] = dden
        grad_query = reach * (
            dot_three(dot_nt, dnum, dlow, state_high, state_low) + dden * total
        )
        grad_key = jnp.zeros((CHUNK, LANES), f32)
        grad_value = jnp.zeros((CHUNK, LANES), f32)
        for index in range(EACH):
            mask = masks[index]
            column = dden[:, index * HEAD : index * HEAD + 1]
            slope = dot_three(dot_nt, dnum, dlow, value * mask, value_low * mask) + column
            high, low = halves(jnp.where(causal, slope, 0.0))
            grad_query = grad_query + dot_nn(high, key * mask) + dot_nn(low, key * mask)
            part_query = query * mask
            grad_key = grad_key + dot_tn(
                jnp.concatenate([high, low], 0), jnp.concatenate([part_query, part_query], 0)
            )
            both = dot_tn(scores[index], jnp.concatenate([dnum * mask, dlow * mask], 1))
            grad_value = grad_value + both[:, :LANES] + both[:, LANES:]
        dk_ref[here, :] = grad_key
        dv_ref[here, :] = grad_value
        grad = phi_back(grad_query, query.astype(f32), uq_ref[here, :].astype(f32), const_ref)
        grad = turn_back(grad, table_ref.at[:, here, :]).astype(bf16)
        dq_ref[here, :] = grad
        bias = bias + jnp.sum(grad.astype(f32), 0, keepdims=True)
        if c < count - 1:
            kept = key.astype(f32) * tail
            kept_low = kept.astype(bf16)
            state = keep * state + blocks * (dot_tn(kept_low, value) + dot_tn(kept_low, value_low))
            total = keep * total + jnp.sum(kept, 0, keepdims=True)
    bias_ref[...] = jnp.broadcast_to(bias, (8, LANES))
    grad_state = jnp.zeros((LANES, LANES), f32)
    grad_total = jnp.zeros((1, LANES), f32)
    for c in reversed(range(count)):
        here = pl.ds(c * CHUNK, CHUNK)
        segment = twice(table_ref[3, here, :])
        before, final = marks_ref[c : c + 1, :], marks_ref[8 + c : 9 + c, :]
        reach = jnp.where(segment == before, 1.0, 0.0)
        tail = jnp.where(segment == final, 1.0, 0.0)
        keep = jnp.where(final == before, 1.0, 0.0)
        if c < count - 1:
            high, low = halves(grad_state)
            dk_ref[here, :] += tail * (
                dot_three(dot_nt, v_ref[here, :], vl_ref[here, :], high, low) + grad_total
            )
            dv_ref[here, :] += tail * (dot_nn(k_ref[here, :], high) + dot_nn(k_ref[here, :], low))
        reached = q_ref[here, :].astype(f32) * reach
        low_reached = reached.astype(bf16)
        grad_state = keep * grad_state + blocks * (
            dot_tn(low_reached, dnum_ref[here, :]) + dot_tn(low_reached, dlow_ref[here, :])
        )
        grad_total = keep * grad_total + jnp.sum(reached * dden_ref[here, :], 0, keepdims=True)
    ds_ref[0:HEAD, :] = squeeze_state(grad_state)
    ds_ref[HEAD:STATE, :] = jnp.broadcast_to(grad_total, (8, LANES))
    mixed = mixed_ref[...]
    accumulate(out_ref, dot_nn(mixed, merge))
    part_owners(dot_tn(mixed, g_ref[...]), core_ref, send_ref, keep_ref)


def accumulate(ref, value):
    first = pl.program_id(0) == 0

    @pl.when(first)
    def _():
        ref[...] = value

    @pl.when(jnp.logical_not(first))
    def _():
        ref[...] += value


def part_owners(value, core_ref, send_ref, keep_ref):
    held = send_ref.shape
    pairs = value.reshape((held[0], 2) + held[1:]).astype(send_ref.dtype)
    even, odd = pairs[:, 0], pairs[:, 1]
    first = core_ref[0] == 0
    keep, send = jnp.where(first, even, odd), jnp.where(first, odd, even)
    keep_ref[...], send_ref[...] = keep, send


def finish_kernel(far, *refs):
    state_refs, refs = refs[:far], refs[far:]
    (
        k_ref, v_ref, vl_ref, uk_ref, dq_ref, dk_ref, dv_ref, weigh_ref, table_ref, marks_ref,
        const_ref, wq_ref, wk_ref, wv_ref, ht_ref, core_ref, _, _, _,
        bias_ref, dh_ref, send_ref, keep_ref,
    ) = refs
    came = arrive(state_refs, weigh_ref)
    segment = twice(table_ref[3])
    tail = jnp.where(segment == marks_ref[15:16, :], 1.0, 0.0)
    high, low = halves(spread(came, const_ref))
    key, value = k_ref[...], v_ref[...]
    grad_key = dk_ref[...] + tail * (
        dot_three(dot_nt, value, vl_ref[...], high, low) + came[HEAD : HEAD + 1, :]
    )
    grad_value = dv_ref[...] + tail * (dot_nn(key, high) + dot_nn(key, low))
    grad = phi_back(grad_key, key.astype(f32), uk_ref[...].astype(f32), const_ref)
    grad = turn_back(grad, table_ref).astype(bf16)
    low_value = grad_value.astype(bf16)
    bias_ref[0:8, :] = jnp.broadcast_to(jnp.sum(grad.astype(f32), 0, keepdims=True), (8, LANES))
    bias_ref[8:16, :] = jnp.broadcast_to(
        jnp.sum(low_value.astype(f32), 0, keepdims=True), (8, LANES)
    )
    grads = (dq_ref[...], grad, low_value)
    weights = (flat(wq_ref[...]), flat(wk_ref[...]), flat(wv_ref[...]))
    accumulate(dh_ref, sum(dot_nt(g, w) for g, w in zip(grads, weights)))
    first = core_ref[0] == 0
    for index, value in enumerate(grads):
        pairs = dot_nn(ht_ref[...], value).reshape(-1, 2, send_ref.shape[2], LANES)
        keep_ref[:, index] = jnp.where(first, pairs[:, 0], pairs[:, 1])
        send_ref[:, index] = jnp.where(first, pairs[:, 1], pairs[:, 0])


def normal_cdf(value):
    bell = jnp.exp(-0.5 * value * value)
    near = jnp.abs(value) * (0.3275911 * math.sqrt(0.5)) + 1.0
    guess = pl.reciprocal(near, approx=True)
    t = guess * (2.0 - near * guess)
    poly = 0.5 * 1.061405429
    for factor in (-1.453152027, 1.421413741, -0.284496736, 0.254829592):
        poly = poly * t + 0.5 * factor
    tail = poly * t * bell
    return jnp.where(value >= 0.0, 1.0 - tail, tail), bell


def feed_kernel(
    h_ref, ht_ref, g_ref, we_ref, ws_ref, be_ref, core_ref, done_ref,
    out_ref, dh_ref, bias_ref, *grad_refs,
):
    step = pl.program_id(0)
    grad_out, rows_in, flipped = g_ref[...], h_ref[...], ht_ref[...]
    expand, shrink = flat(we_ref[...]), flat(ws_ref[...])
    width = expand.shape[1]
    half = width // 2
    _, blocks, rows, _ = grad_refs[0].shape
    block = step // (D // width)
    first = core_ref[0] == 0

    def products(side):
        cut = slice(side * half, (side + 1) * half)
        pre = dot_nn(rows_in, expand[:, cut]) + be_ref[:, cut]
        return pre, dot_nt(grad_out, shrink[cut])

    def pointwise(side, pre, grad):
        cdf, bell = normal_cdf(pre)
        active = (pre * cdf).astype(bf16)
        slope = cdf + pre * bell * (1.0 / math.sqrt(2.0 * math.pi))
        grad = (grad * slope).astype(bf16)
        bias_ref[:, side * half : (side + 1) * half] = jnp.broadcast_to(
            jnp.sum(grad.astype(f32), 0, keepdims=True), (8, half)
        )
        return active, grad

    def gradients(side, active, grad):
        start = lax.rem(step, D // width) * width + side * half
        lanes = pl.ds(pl.multiple_of(start, half), half)
        wide = dot_nn(flipped, grad).astype(bf16)
        tall = dot_tn(active, grad_out).astype(bf16).reshape(blocks // 2, rows, D)
        if len(grad_refs) == 1:
            grad_refs[0][:, block, :, lanes] = wide.reshape(-1, rows, half)
            grad_refs[0][2 * step + side, blocks // 2 :] = tall
        else:
            send_ref, keep_ref = grad_refs
            pairs = wide.reshape(-1, 2, rows, half)
            keep_ref[:, block, :, lanes] = jnp.where(first, pairs[:, 0], pairs[:, 1])
            send_ref[:, block, :, lanes] = jnp.where(first, pairs[:, 1], pairs[:, 0])

            @pl.when(first == (side == 0))
            def _():
                keep_ref[step, blocks // 2 :] = tall

            @pl.when(first != (side == 0))
            def _():
                send_ref[step, blocks // 2 :] = tall

    left = products(0)
    left = pointwise(0, *left)
    right = products(1)
    gradients(0, *left)
    right = pointwise(1, *right)
    forward = dot_nn(left[0], shrink[:half])
    backward = dot_nt(left[1], expand[:, :half])
    gradients(1, *right)
    accumulate(out_ref, forward + dot_nn(right[0], shrink[half:]))
    accumulate(dh_ref, backward + dot_nt(right[1], expand[:, half:]))


def close_kernel(x_ref, g_ref, one_ref, mixed_ref, *refs):
    feeds, (lines_ref, _, out_ref, grad_ref, sums_ref) = refs[:-5], refs[-5:]
    half = len(feeds) // 2
    inputs = x_ref[...].astype(f32)
    result = inputs + mixed_ref[...] + lines_ref[2:3, :]
    out_ref[...] = (result + sum(ref[...] for ref in feeds[:half])).astype(bf16)
    normed, root = layer_parts(inputs)
    one, two = one_ref[...], sum(ref[...] for ref in feeds[half:])
    pulled = one * lines_ref[0:1, :] + two * lines_ref[1:2, :]
    drop = jnp.mean(pulled, -1, keepdims=True)
    lean = jnp.mean(pulled * normed, -1, keepdims=True)
    outer = g_ref[...].astype(f32)
    grad_ref[...] = (outer + root * (pulled - drop - normed * lean)).astype(bf16)
    values = (one * normed, one, two * normed, two, outer)
    rows = [jnp.sum(value, 0, keepdims=True) for value in values]
    accumulate(sums_ref, jnp.concatenate(rows + [jnp.zeros((3, D), f32)], 0))


def lamb_step(master, first, second, grad, mean_ref, square_ref, update_ref, norms_ref):
    first, second, update = lamb_update(master, first, second, grad, DECAY)
    mean_ref[...], square_ref[...], update_ref[...] = first, second, update
    for index, value in enumerate((master, update)):
        squares = jnp.sum((value * value).reshape(-1, 8, value.shape[-1]), 0)
        accumulate(norms_ref.at[index], squares)


def lamb_feed_kernel(
    ep_ref, em_ref, es_ref, eg_ref, sp_ref, sm_ref, ss_ref, sg_ref, *refs
):
    enorm_ref, snorm_ref, *outs = refs[-8:]
    lamb_step(ep_ref[...], em_ref[...], es_ref[...], eg_ref[0].astype(f32), *outs[:3], enorm_ref)
    lamb_step(sp_ref[...], sm_ref[...], ss_ref[...], sg_ref[...].astype(f32), *outs[3:], snorm_ref)


def lamb_attend_kernel(
    ap_ref, am_ref, as_ref, mp_ref, mm_ref, ms_ref, grad_ref,
    anorm_ref, mnorm_ref, *outs,
):
    step = pl.program_id(0)
    grad = grad_ref[step].astype(f32)
    grad = grad + jnp.where(step < 2, grad_ref[jnp.minimum(4 + step, 5)].astype(f32), 0.0)
    lamb_step(ap_ref[...], am_ref[...], as_ref[...], grad, *outs[:3], anorm_ref)

    @pl.when(step == 0)
    def _():
        grad = grad_ref[3].astype(f32)
        lamb_step(mp_ref[...], mm_ref[...], ms_ref[...], grad, *outs[3:], mnorm_ref)


def renew_kernel(squares_ref, *refs):
    count = len(refs) // 3
    for index in range(count):
        master_ref, update_ref, fresh_ref = refs[2 * index], refs[2 * index + 1], refs[2 * count + index]
        lanes = (1, master_ref.shape[-1])
        weight = jnp.sqrt(jnp.full(lanes, squares_ref[2 * index], f32))
        change = jnp.sqrt(jnp.full(lanes, squares_ref[2 * index + 1], f32))
        ratio = RATE * (weight / (change + EPSILON))
        fresh_ref[...] = master_ref[...] - ratio * update_ref[...]


def whole(shape):
    return pl.BlockSpec(shape, lambda g: (0,) * len(shape), pipeline_mode=pl.Buffered(1))


def total_of(shape):
    return pl.BlockSpec(shape, lambda g: (0,) * len(shape))


def scalar():
    return pl.BlockSpec(memory_space=pltpu.SMEM)


def columns(rows, width=LANES, offset=0):
    return pl.BlockSpec((rows, width), lambda g: (0, g + offset))


def shaped(shape, dtype):
    return jax.ShapeDtypeStruct(shape, dtype)


def params():
    return pltpu.CompilerParams(vmem_limit_bytes=ROOM, dimension_semantics=("arbitrary",))


def layer_parts(inputs):
    center = inputs - jnp.mean(inputs, -1, keepdims=True)
    spread_of = jnp.mean(center * center, -1, keepdims=True)
    root = lax.rsqrt(spread_of + 1e-05)
    return center * root, root


def lamb_update(master, first, second, grad, decay):
    first = BETA_ONE * first + (1.0 - BETA_ONE) * grad
    second = BETA_TWO * second + (1.0 - BETA_TWO) * grad * grad
    update = (
        first / (1.0 - BETA_ONE**STEP) / (jnp.sqrt(second / (1.0 - BETA_TWO**STEP)) + EPSILON)
        + decay * master
    )
    return (first, second, update)


def per_device(
    tokens,
    cotangent,
    lengths,
    attend_weight,
    merge_weight,
    expand_weight,
    shrink_weight,
    gains_biases,
    attend_first,
    attend_second,
    merge_first,
    merge_second,
    expand_first,
    expand_second,
    shrink_first,
    shrink_second,
    vector_first,
    vector_second,
):
    rows = tokens.shape[1]
    count = rows // CHUNK
    n = lax.axis_size("seq")
    device = lax.axis_index("seq")
    grad_out = cotangent[0]
    own = D // n
    parts = 2 if FF // n >= 256 else 1
    sub = FF // n // parts
    tall = FF // D // parts
    core = lax.rem(device, 2)
    core_ref = core[None].astype(jnp.int32)

    def gather(blocks):
        shard = jnp.concatenate([block.astype(bf16) for block in blocks], 0)
        full = lax.all_gather(shard, "seq", axis=0, tiled=False)
        return full.reshape(n, shard.shape[0] // own, own, D)

    def of_part(array, index):
        return jnp.concatenate(
            [array[:, (j * parts + index) * sub : (j * parts + index + 1) * sub] for j in range(n)], 1
        )

    attend = gather([attend_weight[:, :D], attend_weight[:, D : 2 * D], attend_weight[:, 2 * D :]])
    merge = gather([merge_weight])
    feeds = []
    for index in range(parts):
        wide = of_part(expand_weight, index)
        feeds.append(
            gather(
                [wide[:, c * D : (c + 1) * D] for c in range(tall)]
                + [shrink_weight[index * sub : (index + 1) * sub]]
            )
        )
    packed = lax.all_gather(gains_biases.astype(bf16), "seq", axis=0, tiled=True)
    vector = packed.astype(f32)
    gain_one = vector[0:D]
    shift_one = vector[D : 2 * D]
    gain_two = vector[2 * D : 3 * D]
    shift_two = vector[3 * D : 4 * D]
    bias_attend = vector[4 * D : 7 * D]
    bias_merge = vector[7 * D : 8 * D]
    bias_expand = vector[8 * D : 8 * D + FF]
    bias_shrink = vector[8 * D + FF :]

    bounds = jnp.cumsum(lengths[0])

    def label(place):
        return jnp.sum((bounds <= place[..., None]).astype(jnp.int32), -1)

    positions = device * rows + jnp.arange(rows, dtype=jnp.int32)
    segment = label(positions)
    starts = jnp.sum(jnp.where(bounds[None, :] <= positions[:, None], lengths[0][None, :], 0), -1)
    offset = positions - starts
    edges = device * rows + jnp.arange(count, dtype=jnp.int32) * CHUNK
    before = jnp.zeros((8,), jnp.int32).at[:count].set(label(edges - 1))
    final = jnp.zeros((8,), jnp.int32).at[:count].set(label(edges + CHUNK - 1))
    final = final.at[7].set(segment[-1])
    marks = jnp.broadcast_to(jnp.concatenate([before, final])[:, None], (16, LANES)).astype(f32)
    halfway = ROT // 2
    inverse = jnp.exp(jnp.arange(halfway, dtype=f32) * (-2.0 * math.log(BASE) / ROT))
    angles = offset.astype(f32)[:, None] * inverse
    cosine, sines = jnp.cos(angles), jnp.sin(angles)
    rest = jnp.ones((rows, HEAD - ROT), f32)
    none = jnp.zeros((rows, HEAD - ROT), f32)
    part = jnp.zeros((rows, halfway), f32)
    table = jnp.stack(
        [
            jnp.tile(jnp.concatenate([cosine, cosine, rest], 1), (1, 2)),
            jnp.tile(jnp.concatenate([-sines, part, none], 1), (1, 2)),
            jnp.tile(jnp.concatenate([part, sines, none], 1), (1, 2)),
            jnp.broadcast_to(segment.astype(f32)[:, None], (rows, 2 * HEAD)),
        ]
    )
    row_table = jnp.broadcast_to(segment.astype(f32)[None, :], (8, rows))
    const_np, weight_np = group_tables()
    const, weighting = jnp.asarray(const_np), jnp.asarray(weight_np)

    inputs = tokens[0].astype(f32)
    normed, root = layer_parts(inputs)
    low_one = (normed * gain_one + shift_one).astype(bf16)
    low_two = (normed * gain_two + shift_two).astype(bf16)

    flipped_one = lax.optimization_barrier(low_one.T)
    flipped_two = lax.optimization_barrier(low_two.T)

    def feed(index, done, parted):
        width = 2 * sub
        per = D // width
        held = (n // 2 if parted else n, 2 * tall, own, D)
        many = 2 if parted else 1
        return pl.pallas_call(
            feed_kernel,
            grid=(n // 2,),
            in_specs=[
                whole((rows, D)),
                whole((D, rows)),
                whole((rows, D)),
                pl.BlockSpec((n, 1, own, width), lambda g: (0, g // per, 0, g % per)),
                pl.BlockSpec((2, tall, own, D), lambda g: (g, 1, 0, 0)),
                pl.BlockSpec((1, width), lambda g: (0, g)),
                scalar(),
                pl.BlockSpec(memory_space=pl.ANY),
            ],
            out_specs=[
                total_of((rows, D)),
                total_of((rows, D)),
                pl.BlockSpec((8, width), lambda g: (0, g)),
                *[total_of(held)] * many,
            ],
            out_shape=[
                shaped((rows, D), f32),
                shaped((rows, D), f32),
                shaped((8, FF // parts), f32),
                *[shaped(held, bf16)] * many,
            ],
            compiler_params=params(),
            cost_estimate=pl.CostEstimate(
                flops=24 * rows * D * FF // parts,
                bytes_accessed=10 * D * FF // parts,
                transcendentals=rows * FF // parts,
            ),
            name="feed",
        )(
            low_two, flipped_two, grad_out, feeds[index], feeds[index],
            of_part(bias_expand[None, :], index), core_ref, done,
        )

    def projection(index):
        return pl.BlockSpec((n, 1, own, LANES), lambda g: (0, index, 0, g))

    constants = [whole((3, LANES, LANES)), whole((1, LANES))]
    tables = [whole((4, rows, 2 * HEAD)), whole((16, LANES))]
    biases = bias_attend.reshape(3, D)
    key, value, value_low, turned_key, summary = pl.pallas_call(
        key_kernel,
        grid=(NGROUP,),
        in_specs=[
            whole((rows, D)),
            *[projection(index) for index in range(1, 3)],
            columns(3),
            *tables,
            *constants,
        ],
        out_specs=[columns(rows)] * 4 + [columns(STATE)],
        out_shape=[shaped((rows, D), bf16)] * 4 + [shaped((STATE, D), f32)],
        compiler_params=params(),
        cost_estimate=pl.CostEstimate(
            flops=4 * rows * D * D + 14 * rows * D * LANES,
            bytes_accessed=14 * rows * D,
            transcendentals=rows * D,
        ),
        name="keys",
    )(low_one, attend, attend, biases, table, marks, const, weighting)
    query, turned_query = pl.pallas_call(
        query_kernel,
        grid=(NGROUP,),
        in_specs=[
            whole((rows, D)),
            projection(0),
            columns(3),
            tables[0],
            *constants,
            pl.BlockSpec(memory_space=pl.ANY),
        ],
        out_specs=[columns(rows)] * 2,
        out_shape=[shaped((rows, D), bf16)] * 2,
        compiler_params=params(),
        cost_estimate=pl.CostEstimate(
            flops=2 * rows * D * D + 8 * rows * D * LANES,
            bytes_accessed=8 * rows * D,
            transcendentals=rows * D,
        ),
        name="queries",
    )(low_one, attend, biases, table, const, weighting, summary)

    reaches = range(1, n // 2 + 1)
    own_before, own_final = label(device * rows - 1), segment[-1]
    carried, weights = [], []
    for far in reaches:
        carried.append(lax.ppermute(summary, "seq", [(e, e + far) for e in range(n - far)]))
        same = (device >= far) & (label((device - far + 1) * rows - 1) == own_before)
        weights.append(same.astype(f32))

    grad_query, part_key, part_value, grad_carried, query_bias, attend_out, send, keep = pl.pallas_call(
        functools.partial(attend_kernel, len(carried)),
        grid=(NGROUP,),
        in_specs=[
            *[columns(STATE)] * len(carried),
            *[columns(rows)] * 5,
            scalar(),
            whole((rows, D)),
            pl.BlockSpec((LANES // own, 1, own, D), lambda g: (g, 0, 0, 0)),
            whole((4, rows, 2 * HEAD)),
            whole((8, rows)),
            whole((16, LANES)),
            whole((3, LANES, LANES)),
            scalar(),
        ],
        out_specs=[columns(rows)] * 3
        + [columns(STATE), columns(8), total_of((rows, D))]
        + [pl.BlockSpec((LANES // own // 2, 1, own, D), lambda g: (g, 3, 0, 0))] * 2,
        out_shape=[
            shaped((rows, D), bf16),
            shaped((rows, D), f32),
            shaped((rows, D), f32),
            shaped((STATE, D), f32),
            shaped((8, D), f32),
            shaped((rows, D), f32),
            shaped((n // 2, 4, own, D), f32),
            shaped((n // 2, 4, own, D), f32),
        ],
        scratch_shapes=[pltpu.VMEM((rows, LANES), kind) for kind in (bf16, bf16, bf16, f32)],
        compiler_params=params(),
        cost_estimate=pl.CostEstimate(
            flops=2 * rows * D * D + 150 * rows * D * LANES,
            bytes_accessed=24 * rows * D,
            transcendentals=0,
        ),
        name="attend",
    )(
        *carried, query, key, value, value_low, turned_query, jnp.stack(weights),
        grad_out, merge, table, row_table, marks, const, core_ref,
    )

    returned, weights = [], []
    for far in reaches:
        returned.append(lax.ppermute(grad_carried, "seq", [(e + far, e) for e in range(n - far)]))
        same = (device + far < n) & (label((device + far) * rows - 1) == own_final)
        weights.append(same.astype(f32))
    fed = [feed(0, grad_carried, False)]

    sides = pl.BlockSpec((n // 2, 3, own, LANES), lambda g: (0, 0, 0, g))
    rest_bias, grad_one, send, keep = pl.pallas_call(
        functools.partial(finish_kernel, len(returned)),
        grid=(NGROUP,),
        in_specs=[columns(STATE)] * len(returned)
        + [columns(rows)] * 7
        + [scalar(), *tables, whole((3, LANES, LANES))]
        + [projection(index) for index in range(3)]
        + [whole((D, rows)), scalar()]
        + [pl.BlockSpec(memory_space=pl.ANY)] * 3,
        out_specs=[columns(16), total_of((rows, D)), sides, sides],
        out_shape=[
            shaped((16, D), f32),
            shaped((rows, D), f32),
            shaped((n // 2, 4, own, D), f32),
            shaped((n // 2, 4, own, D), f32),
        ],
        input_output_aliases={16 + len(returned): 2, 17 + len(returned): 3},
        compiler_params=params(),
        cost_estimate=pl.CostEstimate(
            flops=12 * rows * D * D + 24 * rows * D * LANES,
            bytes_accessed=18 * rows * D,
            transcendentals=0,
        ),
        name="finish",
    )(
        *returned, key, value, value_low, turned_key, grad_query, part_key, part_value,
        jnp.stack(weights), table, marks, const, attend, attend, attend, flipped_one, core_ref, send, keep, fed[0][2],
    )
    for index in range(1, parts):
        fed.append(feed(index, rest_bias, True))

    bits = n.bit_length() - 1

    def exchange(array, bit):
        return lax.ppermute(array, "seq", [(i, i ^ (1 << bit)) for i in range(n)])

    def scatter(keep, came):
        middle = keep.shape[1] // 2
        order = list(range(1, bits))
        turned = (bits - 1) // 2
        orders = order, order[turned:] + order[:turned]
        places = order[::-1]
        deep = keep.reshape((2,) * (bits - 1) + keep.shape[1:])
        came = came.reshape(deep.shape)
        sides = [[(deep, places, side * middle), (came, places, side * middle)] for side in range(2)]

        def pick(terms, fixed):
            total = 0.0
            for array, axes, start in terms:
                starts = [fixed.get(bit, 0) for bit in axes] + [start, 0, 0]
                sizes = [1 if bit in fixed else 2 for bit in axes] + [middle, own, D]
                value = lax.dynamic_slice(array, starts, sizes).astype(f32)
                kept = [2 for bit in places if bit not in fixed]
                total = total + value.reshape(kept + [middle, own, D])
            return total

        for place in range(bits - 1):
            for side in range(2):
                bit, earlier = orders[side][place], orders[side][:place]
                fixed = {b: (device >> b) & 1 for b in earlier}
                fixed[bit] = 1 - ((device >> bit) & 1)
                other = pick(sides[side], fixed).astype(bf16)
                left = [b for b in places if b not in fixed]
                sides[side].append((exchange(other, bit), left, 0))
        fixed = {b: (device >> b) & 1 for b in order}
        return jnp.concatenate([pick(terms, fixed) for terms in sides], 0)

    spot = jnp.stack([(device >> 1) & 1, (device >> 2) & 1]).astype(jnp.int32)

    def add_step(terms, outs, done, count):
        flat_terms = [term for group in terms for term in group]
        sizes = [len(group) for group in terms]

        def kernel(spot_ref, *refs):
            ins, out_refs = refs[: len(flat_terms)], refs[len(flat_terms) + len(done) :]
            at = 0
            for size, (out_ref, place) in zip(sizes, count(out_refs)):
                shape = out_ref.at[place].shape
                total = ins[at][...].astype(f32).reshape(shape)
                for ref in ins[at + 1 : at + size]:
                    total = total + ref[...].astype(f32).reshape(shape)
                out_ref[place] = total.astype(out_ref.dtype)
                at += size

        return pl.pallas_call(
            kernel,
            grid_spec=pltpu.PrefetchScalarGridSpec(
                num_scalar_prefetch=1,
                grid=(2,),
                in_specs=[spec for _, spec in flat_terms]
                + [pl.BlockSpec(memory_space=pl.ANY)] * len(done),
                out_specs=[spec for _, spec in outs],
            ),
            out_shape=[shape for shape, _ in outs],
            compiler_params=params(),
            name="add",
        )(spot, *[array for array, _ in flat_terms], *done)

    one, two = (1, 1, 1, own, D), (1, 1, 2, own, D)

    def step_one(keep, came, done):
        wide = pl.BlockSpec(two, lambda g, at: (g, 1 - at[0], 0, 0, 0))
        tall_part = pl.BlockSpec(two, lambda g, at: (1 - at[1], g, 1, 0, 0))
        out = shaped((2, 2, own, D), bf16), pl.BlockSpec((1, 2, own, D), lambda g, at: (g, 0, 0, 0))
        terms = [[(keep, wide), (came, wide)], [(keep, tall_part), (came, tall_part)]]
        first, second = add_step(terms, [out] * 2, done, lambda refs: [(ref, ...) for ref in refs])
        return first, exchange(first, 1), exchange(second, 2)

    def step_two(keep, came, first, second, done):
        wide = pl.BlockSpec(one, lambda g, at: (1 - at[1], at[0], g, 0, 0))
        tall_part = pl.BlockSpec(one, lambda g, at: (at[1], 1 - at[0], 2 + g, 0, 0))
        first_of = pl.BlockSpec((1, 1, own, D), lambda g, at: (1 - at[1], g, 0, 0))
        second_of = pl.BlockSpec((1, 1, own, D), lambda g, at: (1 - at[0], g, 0, 0))
        out = shaped((2, own, D), bf16), pl.BlockSpec((1, own, D), lambda g, at: (g, 0, 0))
        terms = [
            [(keep, wide), (came, wide), (first, first_of)],
            [(keep, tall_part), (came, tall_part), (second, second_of)],
        ]
        sent = add_step(terms, [out] * 2, done, lambda refs: [(ref, ...) for ref in refs])
        return exchange(sent[0], 2), exchange(sent[1], 1)

    def step_three(keep, came, first, second, last_first, last_second, kind, done):
        wide = pl.BlockSpec(one, lambda g, at: (at[1], at[0], g, 0, 0))
        tall_part = pl.BlockSpec(one, lambda g, at: (at[1], at[0], 2 + g, 0, 0))
        first_of = pl.BlockSpec((1, 1, own, D), lambda g, at: (at[1], g, 0, 0))
        second_of = pl.BlockSpec((1, 1, own, D), lambda g, at: (at[0], g, 0, 0))
        last = pl.BlockSpec((1, own, D), lambda g, at: (g, 0, 0))
        out = shaped((2, 2, own, D), kind), pl.BlockSpec((2, 1, own, D), lambda g, at: (0, g, 0, 0))
        terms = [
            [(keep, wide), (came, wide), (first, first_of), (last_first, last)],
            [(keep, tall_part), (came, tall_part), (second, second_of), (last_second, last)],
        ]
        result = add_step(terms, [out], done, lambda refs: [(refs[0], 0), (refs[0], 1)])
        return result[0].reshape(4, own, D)

    groups = lax.axis_size("dp")
    group = lax.axis_index("dp")

    def sum_groups(value, fine, begun):
        blocks = value.shape[0]
        shares = value.reshape(blocks, groups, own // groups, D)
        rolls = {far: [(i, (i + far) % groups) for i in range(groups)] for far in range(1, groups)}

        def share(which):
            return lax.dynamic_index_in_dim(shares, which % groups, 1, False)

        total = share(group)
        for far, pairs in rolls.items():
            total = total + lax.ppermute(share(group + far).astype(bf16), "dp", pairs).astype(f32)
        total = total + begun
        high = lax.reduce_precision(total, 8, 7)
        total = jnp.concatenate([high, (total - high)[:fine]], 0).astype(bf16)
        result = jnp.zeros((blocks + fine,) + shares.shape[1:], bf16)
        result = lax.dynamic_update_index_in_dim(result, total, group, 1)
        for far, pairs in rolls.items():
            came = lax.ppermute(total, "dp", pairs)
            result = lax.dynamic_update_index_in_dim(result, came, (group - far) % groups, 1)
        return result.reshape(blocks + fine, own, D), total

    def sum_all(value):
        for bit in range(bits):
            value = value + exchange(value, bit)
        for bit in range(groups.bit_length() - 1):
            pairs = [(i, i ^ (1 << bit)) for i in range(groups)]
            value = value + lax.ppermute(value, "dp", pairs)
        return value

    first_part = lax.psum_scatter(fed[0][3], "seq", scatter_dimension=0, tiled=False)
    feed_sums = [lax.psum(first_part, "dp")]
    if bits == 3 and parts == 2:
        deep = (2, 2, 4, own, D)
        feed_send, feed_keep = (array.reshape(deep) for array in fed[1][3:])
        feed_came = exchange(feed_send, 0)
        send, keep = send.reshape(deep), keep.reshape(deep)
        came = exchange(send, 0)
        started, *first = step_one(keep, came, [fed[1][2], first_part])
        arrived = first[0]
        begun, *feed_first = step_one(feed_keep, feed_came, [started])
        second = step_two(keep, came, *first, [begun])
        feed_second = step_two(feed_keep, feed_came, *feed_first, [])
        attend_part = step_three(
            keep, came, *first, *second, f32, [*feed_second, feed_sums[0]]
        )
        feed_part = step_three(
            feed_keep, feed_came, *feed_first, *feed_second, bf16, [attend_part]
        )
        feed_sums.append(lax.psum(feed_part, "dp"))
        feed_sums_begun = 0.0 * feed_part[0, 0, 0].astype(f32)
    else:
        for index in range(1, parts):
            part = scatter(fed[index][4], exchange(fed[index][3], 0))
            feed_sums.append(lax.psum(part.astype(bf16), "dp"))
        attend_part = scatter(keep, exchange(send, 0))
        feed_sums_begun, arrived = 0.0, attend_part
    attend_sum, attend_share = sum_groups(attend_part, 2, feed_sums_begun)

    strip = pl.BlockSpec((128, D), lambda g: (g, 0))
    lines = jnp.stack([gain_one, gain_two, bias_merge + bias_shrink] + [gain_one] * 5)
    block_output, input_grad, sums = pl.pallas_call(
        close_kernel,
        grid=(rows // 128,),
        in_specs=[strip] * (4 + 2 * parts) + [whole((8, D)), pl.BlockSpec(memory_space=pl.ANY)],
        out_specs=[strip, strip, total_of((8, D))],
        out_shape=[shaped((rows, D), bf16), shaped((rows, D), bf16), shaped((8, D), f32)],
        compiler_params=params(),
        name="close",
    )(
        tokens[0], grad_out, grad_one, attend_out, *[f[0] for f in fed], *[f[1] for f in fed],
        lines, arrived,
    )
    block_output, input_grad = block_output[None], input_grad[None]
    feed_bias = jnp.concatenate(
        [fed[p][2][0, j * sub : (j + 1) * sub] for j in range(n) for p in range(parts)]
    )
    grad_vector = jnp.concatenate(
        [sums[0:4].reshape(-1), query_bias[0], rest_bias[0], rest_bias[8], sums[4], feed_bias, sums[4]]
    )
    grad_vector = grad_vector + 0.0 * attend_sum[0, 0, 0].astype(f32)
    vector_sum = sum_all(grad_vector.reshape(-1, 128)).reshape(-1)
    share = gains_biases.shape[0]
    own_vector = lax.dynamic_slice(vector_sum, (device * share,), (share,))

    strips = 8

    wide_cols = FF // parts // strips
    per = D // wide_cols
    held = None
    expand_sums, shrink_sums = [], []
    for index in range(parts):
        of_expand = pl.BlockSpec((own, wide_cols), lambda g: (0, g * parts + index))
        of_shrink = pl.BlockSpec((sub // strips, D), lambda g: (index * strips + g, 0))
        before_specs = [] if held is None else [pl.BlockSpec(memory_space=pl.ANY)] * 6
        expand_norm, shrink_norm, *held = pl.pallas_call(
            lamb_feed_kernel,
            grid=(strips,),
            in_specs=[of_expand] * 3
            + [pl.BlockSpec((1, own, wide_cols), lambda g: (g // per, 0, g % per))]
            + [of_shrink] * 3
            + [pl.BlockSpec((sub // strips, D), lambda g: (strips + g, 0))]
            + (before_specs or [pl.BlockSpec(memory_space=pl.ANY)]),
            out_specs=[total_of((2, 8, wide_cols)), total_of((2, 8, D))]
            + [of_expand] * 3
            + [of_shrink] * 3,
            out_shape=[shaped((2, 8, wide_cols), f32), shaped((2, 8, D), f32)]
            + [shaped((own, FF), f32)] * 3
            + [shaped((FF // n, D), f32)] * 3,
            input_output_aliases={} if held is None else {8 + i: 2 + i for i in range(6)},
            compiler_params=params(),
            name="lamb_feed",
        )(
            expand_weight, expand_first, expand_second, feed_sums[index],
            shrink_weight, shrink_first, shrink_second, flat(feed_sums[index]),
            *([attend_share] if held is None else held),
        )
        expand_sums.append(jnp.sum(expand_norm, (1, 2)))
        shrink_sums.append(jnp.sum(shrink_norm, (1, 2)))
    expand_mean, expand_square, expand_update, shrink_mean, shrink_square, shrink_update = held
    block_of = pl.BlockSpec((own, D), lambda g: (0, g))
    attend_norm, merge_norm, *held = pl.pallas_call(
        lamb_attend_kernel,
        grid=(3,),
        in_specs=[block_of] * 3 + [whole((own, D))] * 3 + [whole((6, own, D))],
        out_specs=[total_of((2, 8, D))] * 2 + [block_of] * 3 + [total_of((own, D))] * 3,
        out_shape=[shaped((2, 8, D), f32)] * 2
        + [shaped((own, 3 * D), f32)] * 3
        + [shaped((own, D), f32)] * 3,
        compiler_params=params(),
        name="lamb_attend",
    )(
        attend_weight, attend_first, attend_second, merge_weight, merge_first, merge_second,
        attend_sum,
    )
    attend_mean, attend_square, attend_update, merge_mean, merge_square, merge_update = held
    vector_mean, vector_square, vector_update = lamb_update(
        gains_biases, vector_first, vector_second, own_vector, 0.0
    )
    local = jnp.concatenate(
        [
            jnp.sum(attend_norm, (1, 2)),
            jnp.sum(merge_norm, (1, 2)),
            sum(expand_sums),
            sum(shrink_sums),
            jnp.stack([jnp.sum(gains_biases * gains_biases), jnp.sum(vector_update * vector_update)]),
        ]
    )
    squares = lax.psum(local, "seq")
    fresh = pl.pallas_call(
        renew_kernel,
        grid=(4,),
        in_specs=[scalar()]
        + [pl.BlockSpec((own, 3 * D // 4), lambda g: (0, g))] * 2
        + [pl.BlockSpec((own, D // 4), lambda g: (0, g))] * 2
        + [pl.BlockSpec((own, FF // 4), lambda g: (0, g))] * 2
        + [pl.BlockSpec((FF // n // 4, D), lambda g: (g, 0))] * 2,
        out_specs=[
            pl.BlockSpec((own, 3 * D // 4), lambda g: (0, g)),
            pl.BlockSpec((own, D // 4), lambda g: (0, g)),
            pl.BlockSpec((own, FF // 4), lambda g: (0, g)),
            pl.BlockSpec((FF // n // 4, D), lambda g: (g, 0)),
        ],
        out_shape=[
            shaped((own, 3 * D), f32),
            shaped((own, D), f32),
            shaped((own, FF), f32),
            shaped((FF // n, D), f32),
        ],
        compiler_params=params(),
        name="renew",
    )(
        squares, attend_weight, attend_update, merge_weight, merge_update,
        expand_weight, expand_update, shrink_weight, shrink_update,
    )
    roots = jnp.sqrt(squares.reshape(5, 2).T.reshape(10))
    vector_fresh = gains_biases - RATE * (roots[4] / (roots[9] + EPSILON)) * vector_update
    return (
        block_output, input_grad,
        fresh[0], attend_mean, attend_square,
        fresh[1], merge_mean, merge_square,
        fresh[2], expand_mean, expand_square,
        fresh[3], shrink_mean, shrink_square,
        vector_fresh, vector_mean, vector_square,
        roots,
    )


def solution(mesh):
    matrix, line = P("seq", None), P("seq")
    stream = P("dp", "seq", None)
    return jax.shard_map(
        per_device,
        mesh=mesh,
        in_specs=(stream, stream, P("dp", None))
        + (matrix,) * 4
        + (line,)
        + (matrix,) * 8
        + (line,) * 2,
        out_specs=(stream, stream) + (matrix,) * 12 + (line,) * 3 + (P(),),
        check_vma=False,
    )
```
